32 devices in a mesh: blk: 4 (over y, x), fsdp: 8 (over z, core).
Axes of the slice: x: 2, y: 2, z: 4, core: 2. Of those that a mesh axis runs over, the one named last changes fastest.
Arguments:
- tokens: bfloat16 [4, 4096, 2048], P('blk', 'fsdp'), may hold values from -21 to 21
- student_weight: float32 [4, 2560, 2048], P('blk', 'fsdp'), may hold values from -0.125 to 0.125
- snapshot: bfloat16 [4, 2560, 2048], P('blk', 'fsdp'), may hold values from -0.125 to 0.125
- moment_one: float32 [4, 2560, 2048], P('blk', 'fsdp'), may hold values from -0.6 to 0.6
- moment_two: float32 [4, 2560, 2048], P('blk', 'fsdp'), may hold values from 0.001 to 0.1
Outputs:
- new_weight: float32 [4, 2560, 2048], P('blk', 'fsdp')
- new_moment_one: float32 [4, 2560, 2048], P('blk', 'fsdp')
- new_moment_two: float32 [4, 2560, 2048], P('blk', 'fsdp')
The draws below stay inside these ranges and needn't reach their ends.
All inputs are finite; a program needn't handle non-finite values.
Results may differ from the reference program's by a relative error of at most 0.0045.
The reference program's roundings to bfloat16 on the way count: a program that leaves them out, or rounds other values in their place, can miss the bound.
Values may be sent and summed in bfloat16 or wider, within the bound.
A program may use at most 128 MiB of HBM per device.

```python
import math
import jax
import jax.numpy as jnp
from jax import lax

D = 2048
HEADS = 16
KVH = 4
HD = 128
SEQ = 256
STEP = 100
QKC = 2560
GROUPS = 4
GROUP_TOKENS = 4096


def draw_tokens(key, part):
    key = jax.random.fold_in(key, 11)
    key_base = jax.random.fold_in(key, 0)
    shape = (GROUPS, GROUP_TOKENS, D)
    values = jnp.clip(jax.random.normal(key_base, shape, jnp.float32), -6.0, 6.0)
    return values.astype(jnp.bfloat16)


def levels(own_key, extent, shards, low, largest):
    gain, own = 1.0, jax.random.fold_in(own_key, 6)
    for axis_at, blocks in shards:
        steps = jnp.exp(jax.random.uniform(jax.random.fold_in(own, axis_at), (blocks,), jnp.float32, low / len(shards), largest / len(shards)))
        gain = gain * jnp.repeat(steps, extent[axis_at] // blocks).reshape([-1 if axis == axis_at else 1 for axis in range(len(extent))])
    return gain


def scatter_about(own_key, extent, deviation, bound, cuts=(), held_as=jnp.bfloat16):
    factor_of = levels(own_key, extent, cuts, -0.22, 0.18) if cuts else 1.0
    values = jax.random.normal(own_key, extent, jnp.float32) * deviation * factor_of
    return jnp.minimum(jnp.maximum(values, -bound), bound).astype(held_as)


def setup_inputs(seed: int = 0) -> dict:
    arg_keys = jax.random.split(jax.random.key(seed), 6)
    return {
        "tokens": draw_tokens(jax.random.fold_in(arg_keys[5], 71), 0),
        "student_weight": scatter_about(arg_keys[1], (GROUPS, QKC, D), D ** -0.5, 0.125, ((0, 4), (1, 8)), jnp.float32),
        "snapshot": scatter_about(arg_keys[2], (GROUPS, QKC, D), D ** -0.5, 0.125, ((0, 4), (1, 8))),
        "moment_one": scatter_about(arg_keys[3], (GROUPS, QKC, D), 0.1, 0.6, ((0, 4), (1, 8)), jnp.float32),
        "moment_two": jnp.clip(jnp.exp(math.log(0.1) - 4.6051702 * jax.random.uniform(arg_keys[4], (GROUPS, QKC, D), jnp.float32) ** levels(arg_keys[4], (GROUPS, QKC, D), ((0, 4), (1, 8)), -0.2, 0.2)), 0.001, 0.1),
    }


THETA = 500000.0
BETA_ONE = 0.9
BETA_TWO = 0.95
LEARN_RATE = 0.002
DECAY = 0.1
EPSILON = 1e-08
MASKED = -1e+30

def rotary_tables(row_count, seq_len, head_size):
    positions = (jnp.arange(row_count) % seq_len).astype(jnp.float32)
    exponents = jnp.arange(head_size // 2).astype(jnp.float32) * (2.0 / head_size)
    frequency = THETA ** (-exponents)
    angles = positions[:, None] * frequency[None, :]
    return (jnp.cos(angles)[:, None, :], jnp.sin(angles)[:, None, :])

def rotate(vectors, cosine, sine_table, direction):
    row_count = vectors.shape[0]
    shaped = vectors.reshape(row_count, -1, HD)
    half_size = HD // 2
    front_half = shaped[..., :half_size]
    back_half = shaped[..., half_size:]
    turned = jnp.concatenate([front_half * cosine - direction * back_half * sine_table, back_half * cosine + direction * front_half * sine_table], axis=-1)
    return turned.reshape(row_count, -1)

def score_gradient(qk_student, qk_teacher):
    row_count = qk_student.shape[0]
    seq_count = row_count // SEQ
    group_size = HEADS // KVH
    inv_root = 1.0 / math.sqrt(HD)
    causal = jnp.arange(SEQ)[:, None] >= jnp.arange(SEQ)[None, :]

    def split_heads(packed):
        packed = packed.astype(jnp.float32)
        queries = packed[:, :HEADS * HD].reshape(seq_count, SEQ, KVH, group_size, HD)
        key_rows = packed[:, HEADS * HD:].reshape(seq_count, SEQ, KVH, HD)
        return (queries, key_rows)

    def log_probs(queries, key_rows):
        scores = jnp.einsum('bikrd,bjkd->bkrij', queries, key_rows) * inv_root
        scores = jnp.where(causal, scores, MASKED)
        return jax.nn.log_softmax(scores, axis=-1)
    query_student, key_student = split_heads(qk_student)
    query_teacher, key_teacher = split_heads(qk_teacher)
    spread = jnp.exp(log_probs(query_student, key_student)) - jnp.exp(log_probs(query_teacher, key_teacher))
    rounded = lax.optimization_barrier((jnp.where(causal, spread, 0.0) / HEADS).astype(jnp.bfloat16))
    weights_wide = rounded.astype(jnp.float32)
    query_grad = jnp.einsum('bkrij,bjkd->bikrd', weights_wide, key_student) * inv_root
    key_grad = jnp.einsum('bkrij,bikrd->bjkd', weights_wide, query_student) * inv_root
    return jnp.concatenate([query_grad.reshape(row_count, HEADS * HD), key_grad.reshape(row_count, KVH * HD)], axis=1)

def reference(tokens, student_weight, snapshot, moment_one, moment_two):
    cosine, sine_table = rotary_tables(GROUP_TOKENS, SEQ, HD)
    weight_list = []
    first_list = []
    second_list = []
    for group in range(GROUPS):
        rows_in = tokens[group]
        student_copy = student_weight[group].astype(jnp.bfloat16)
        teacher = snapshot[(group - 1) % GROUPS]
        raw_student = jnp.dot(rows_in, student_copy.T, preferred_element_type=jnp.float32)
        raw_teacher = jnp.dot(rows_in, teacher.T, preferred_element_type=jnp.float32)
        qk_student = lax.optimization_barrier(rotate(raw_student, cosine, sine_table, 1.0).astype(jnp.bfloat16))
        qk_teacher = lax.optimization_barrier(rotate(raw_teacher, cosine, sine_table, 1.0).astype(jnp.bfloat16))
        proj_grad = rotate(score_gradient(qk_student, qk_teacher), cosine, sine_table, -1.0).astype(jnp.bfloat16)
        gradient = jnp.dot(proj_grad.T, rows_in, preferred_element_type=jnp.float32)
        first_new = BETA_ONE * moment_one[group] + (1.0 - BETA_ONE) * gradient
        second_new = BETA_TWO * moment_two[group] + (1.0 - BETA_TWO) * gradient * gradient
        step_dir = first_new / (1.0 - BETA_ONE ** STEP) / (jnp.sqrt(second_new / (1.0 - BETA_TWO ** STEP)) + EPSILON)
        master = student_weight[group]
        weight_list.append(master - LEARN_RATE * (step_dir + DECAY * master))
        first_list.append(first_new)
        second_list.append(second_new)
    return (jnp.stack(weight_list, 0), jnp.stack(first_list, 0), jnp.stack(second_list, 0))
```

```python
import functools
import math

import jax
import jax.numpy as jnp
from jax import lax
from jax.experimental import pallas as pl
from jax.experimental.pallas import tpu as pltpu
from jax.sharding import PartitionSpec as P

HEADS = 16
KVH = 4
HD = 128
SEQ = 256
STEP = 100
GROUP = HEADS // KVH
HEAD_ROWS = (GROUP + 1) * HD
UNITS = GROUP + 1

THETA = 500000.0
BETA_ONE = 0.9
BETA_TWO = 0.95
LEARN_RATE = 0.002
DECAY = 0.1
EPSILON = 1e-08
MASKED = -1e30
MESH = pl.DeviceIdType.MESH


def rotary_tables():
    positions = jnp.arange(SEQ).astype(jnp.float32)
    exponents = jnp.arange(HD // 2).astype(jnp.float32) * (2.0 / HD)
    angles = positions[:, None] * (THETA ** (-exponents))[None, :]
    cosine, sine = jnp.cos(angles), jnp.sin(angles)
    return (
        jnp.concatenate([cosine, cosine], axis=1),
        jnp.concatenate([-sine, sine], axis=1),
    )


def sequence_grad(x, w_student, w_teacher, cosine, sine):
    inv_root = 1.0 / math.sqrt(HD)

    def project(weight):
        raw = lax.dot_general(
            x, weight, (((1,), (1,)), ((), ())), preferred_element_type=jnp.float32
        )
        parts = []
        for head in range(GROUP + 1):
            part = raw[:, head * HD : (head + 1) * HD]
            turned = part * cosine + pltpu.roll(part, HD // 2, 1) * sine
            parts.append(turned.astype(jnp.bfloat16))
        return parts

    student, teacher = project(w_student), project(w_teacher)
    rows = lax.broadcasted_iota(jnp.int32, (SEQ, SEQ), 0)
    columns = lax.broadcasted_iota(jnp.int32, (SEQ, SEQ), 1)
    causal = rows >= columns

    def probs(query, key):
        scores = (
            lax.dot_general(
                query, key, (((1,), (1,)), ((), ())), preferred_element_type=jnp.float32
            )
            * inv_root
        )
        scores = jnp.where(causal, scores, MASKED)
        spread = jnp.exp(scores - jnp.max(scores, axis=-1, keepdims=True))
        return spread * (1.0 / jnp.sum(spread, axis=-1, keepdims=True))

    def turn_back(part):
        return (part * cosine - pltpu.roll(part, HD // 2, 1) * sine).astype(jnp.bfloat16)

    pieces = []
    key_grad = jnp.zeros((SEQ, HD), jnp.float32)
    for head in range(GROUP):
        spread = probs(student[head], student[GROUP]) - probs(teacher[head], teacher[GROUP])
        rounded = (jnp.where(causal, spread, 0.0) * (1.0 / HEADS)).astype(jnp.bfloat16)
        query_grad = jnp.dot(rounded, student[GROUP], preferred_element_type=jnp.float32)
        pieces.append(turn_back(query_grad * inv_root))
        key_grad += lax.dot_general(
            rounded, student[head], (((0,), (0,)), ((), ())), preferred_element_type=jnp.float32
        )
    pieces.append(turn_back(key_grad * inv_root))
    return jnp.concatenate(pieces, axis=1)


def kernel(
    n, blocks, seqs,
    tokens, student, teacher, cos_ref, sin_ref, out,
    held, weight, total, partial,
    w_send, w_recv, s_send, s_recv, t_send, t_recv, g_send, g_recv, f_send, f_recv,
):
    share = n // KVH
    me, blk = lax.axis_index("fsdp"), lax.axis_index("blk")
    chip, lane = lax.div(me, share), lax.rem(me, share)

    def placed(native):
        is_key = lax.div(native, HEADS * share)
        key = (native - HEADS * share) * is_key
        head = (1 - is_key) * lax.div(native, GROUP * share) + is_key * lax.div(key, share)
        at = (1 - is_key) * lax.rem(native, GROUP * share) + is_key * (
            GROUP * share + lax.rem(key, share)
        )
        return head * (UNITS * share) + at

    def native_of(place):
        head, at = lax.div(place, UNITS * share), lax.rem(place, UNITS * share)
        is_key = lax.div(at, GROUP * share)
        return (1 - is_key) * (GROUP * share * head + at) + is_key * (
            HEADS * share + share * head + at - GROUP * share
        )

    def each(count, body):
        def run(step, carry):
            body(step)
            return carry

        lax.fori_loop(0, count, run, 0)

    def landed(ref, sem):
        pltpu.make_async_copy(ref, ref, sem).wait()

    def to(src, dst, send_sem, recv_sem, device, group=None):
        target = {"fsdp": device, "blk": blk if group is None else group}
        return pltpu.make_async_remote_copy(
            src_ref=src, dst_ref=dst, send_sem=send_sem, recv_sem=recv_sem,
            device_id=target, device_id_type=MESH,
        )

    for seq in range(seqs):
        pltpu.make_async_copy(tokens.at[seq], held.at[chip, seq], t_recv.at[chip, seq]).start()

    barrier = pltpu.get_barrier_semaphore()
    after = lax.rem(blk + 1, blocks)
    before = lax.rem(blk + blocks - 1, blocks)

    def greet(step):
        pl.semaphore_signal(
            barrier, inc=1, device_id={"fsdp": lax.rem(me + 1 + step, n), "blk": blk},
            device_id_type=MESH,
        )

    def greet_teacher(unit):
        source = lax.div(native_of(me * UNITS + unit), UNITS)
        pl.semaphore_signal(
            barrier, inc=1, device_id={"fsdp": source, "blk": before}, device_id_type=MESH
        )

    each(n - 1, greet)
    each(UNITS, greet_teacher)
    pl.semaphore_wait(barrier, n - 1 + UNITS)

    def send_rows(unit):
        place = placed(me * UNITS + unit)
        device, slot = lax.div(place, UNITS), lax.rem(place, UNITS)
        at = lax.rem(place, UNITS * share)

        @pl.when(device == me)
        def _():
            pltpu.make_async_copy(
                student.at[unit], weight.at[0, at], w_recv.at[0, slot]
            ).start()

        @pl.when(device != me)
        def _():
            to(
                student.at[unit], weight.at[0, at], w_send.at[0, unit], w_recv.at[0, slot], device
            ).start()

        to(
            teacher.at[unit], weight.at[1, at], w_send.at[1, unit], w_recv.at[1, slot], device,
            after,
        ).start()

    each(UNITS, send_rows)

    def pass_right(src, slot, seq):
        return to(src, held.at[slot, seq], t_send.at[0, slot, seq], t_recv.at[slot, seq], me + share)

    def pass_left(src, slot, seq):
        return to(src, held.at[slot, seq], t_send.at[1, slot, seq], t_recv.at[slot, seq], me - share)

    for seq in range(seqs):

        @pl.when(chip < KVH - 1)
        def _():
            pass_right(tokens.at[seq], chip, seq).start()

        @pl.when(chip > 0)
        def _():
            pass_left(tokens.at[seq], chip, seq).start()

    total[...] = jnp.zeros_like(total)

    def sibling(step):
        return chip * share + lax.rem(lane + step, share)

    for which in range(2):
        each(
            UNITS,
            lambda unit: landed(weight.at[which, lane * UNITS + unit], w_recv.at[which, unit]),
        )
        mine = weight.at[which, pl.ds(lane * UNITS, UNITS)]
        for step in range(1, share):
            to(
                mine, mine, s_send.at[which, step - 1], s_recv.at[which, step - 1], sibling(step)
            ).start()
    for which in range(2):
        for step in range(1, share):
            lane_from = lax.rem(lane + share - step, share)
            landed(
                weight.at[which, pl.ds(lane_from * UNITS, UNITS)], s_recv.at[which, step - 1]
            )

    def work(step):
        seq = lax.rem(step, seqs)
        distance = lax.div(step, 2 * seqs)
        side = lax.rem(lax.div(step, seqs), 2)
        slot = chip - distance + 2 * distance * side
        valid = (distance + 1 - side > 0) & (slot >= 0) & (slot < KVH)

        @pl.when(valid)
        def _():
            landed(held.at[slot, seq], t_recv.at[slot, seq])

            @pl.when((distance > 0) & (side == 0) & (chip < KVH - 1))
            def _():
                pass_right(held.at[slot, seq], slot, seq).start()

            @pl.when((distance > 0) & (side == 1) & (chip > 0))
            def _():
                pass_left(held.at[slot, seq], slot, seq).start()

            x = held[slot, seq]
            grad = sequence_grad(
                x,
                weight[0].reshape(HEAD_ROWS, -1),
                weight[1].reshape(HEAD_ROWS, -1),
                cos_ref[...],
                sin_ref[...],
            )
            width = 512
            for start in range(0, x.shape[1], width):
                piece = lax.dot_general(
                    grad, x[:, start : start + width], (((0,), (0,)), ((), ())),
                    preferred_element_type=jnp.float32,
                )
                total[:, :, start : start + width] += piece.reshape(UNITS * share, -1, width)

    each(2 * KVH * seqs, work)

    def send_partial(unit):
        for step in range(1, share):
            lane_to = lax.rem(lane + step, share)
            to(
                total.at[lane_to * UNITS + unit], partial.at[step - 1, unit],
                g_send.at[step - 1, unit], g_recv.at[step - 1, unit], sibling(step),
            ).start()

    each(UNITS, send_partial)

    def send_sum(unit):
        at = lane * UNITS + unit
        native = native_of(me * UNITS + unit)
        device, slot = lax.div(native, UNITS), lax.rem(native, UNITS)
        for step in range(1, share):
            landed(partial.at[step - 1, unit], g_recv.at[step - 1, unit])
            total[at] += partial[step - 1, unit]

        @pl.when(device == me)
        def _():
            pltpu.make_async_copy(total.at[at], out.at[slot], f_recv.at[slot]).start()

        @pl.when(device != me)
        def _():
            to(total.at[at], out.at[slot], f_send.at[unit], f_recv.at[slot], device).start()

    each(UNITS, send_sum)

    each(UNITS, lambda unit: landed(out.at[unit], f_recv.at[unit]))

    def sent(unit):
        place = placed(me * UNITS + unit)

        @pl.when(lax.div(place, UNITS) != me)
        def _():
            landed(student.at[unit], w_send.at[0, unit])

        landed(teacher.at[unit], w_send.at[1, unit])
        for step in range(1, share):
            landed(partial.at[step - 1, unit], g_send.at[step - 1, unit])

        @pl.when(lax.div(native_of(me * UNITS + unit), UNITS) != me)
        def _():
            landed(out.at[unit], f_send.at[unit])

    each(UNITS, sent)
    for which in range(2):
        for step in range(1, share):
            landed(weight.at[which, pl.ds(lane * UNITS, UNITS)], s_send.at[which, step - 1])

    def sent_tokens(step):
        slot, seq = lax.div(step, seqs), lax.rem(step, seqs)

        @pl.when((slot <= chip) & (chip < KVH - 1))
        def _():
            landed(held.at[slot, seq], t_send.at[0, slot, seq])

        @pl.when((slot >= chip) & (chip > 0))
        def _():
            landed(held.at[slot, seq], t_send.at[1, slot, seq])

    each(KVH * seqs, sent_tokens)


def gradient_rows(tokens, student_copy, snapshot, n, blocks):
    rows, width = student_copy.shape
    seqs = tokens.shape[0] // SEQ
    share = n // KVH
    unit = rows // UNITS
    cosine, sine = rotary_tables()
    dma = pltpu.SemaphoreType.DMA
    anywhere, vmem = pl.BlockSpec(memory_space=pl.ANY), pl.BlockSpec(memory_space=pltpu.VMEM)
    gradient = pl.pallas_call(
        functools.partial(kernel, n, blocks, seqs),
        out_shape=jax.ShapeDtypeStruct((UNITS, unit, width), jnp.float32),
        in_specs=[anywhere, anywhere, anywhere, vmem, vmem],
        out_specs=vmem,
        scratch_shapes=[
            pltpu.VMEM((KVH, seqs, SEQ, width), jnp.bfloat16),
            pltpu.VMEM((2, UNITS * share, unit, width), jnp.bfloat16),
            pltpu.VMEM((UNITS * share, unit, width), jnp.float32),
            pltpu.VMEM((share - 1, UNITS, unit, width), jnp.float32),
            dma((2, UNITS)),
            dma((2, UNITS)),
            dma((2, share - 1)),
            dma((2, share - 1)),
            dma((2, KVH, seqs)),
            dma((KVH, seqs)),
            dma((share - 1, UNITS)),
            dma((share - 1, UNITS)),
            dma((UNITS,)),
            dma((UNITS,)),
        ],
        compiler_params=pltpu.CompilerParams(
            collective_id=0, has_side_effects=True, vmem_limit_bytes=56 * 1024 * 1024
        ),
    )(
        tokens.reshape(seqs, SEQ, width),
        student_copy.reshape(UNITS, unit, width),
        snapshot.reshape(UNITS, unit, width),
        cosine,
        sine,
    )
    return gradient.reshape(rows, width)


def per_device(n, blocks, tokens, student_weight, snapshot, moment_one, moment_two):
    master = student_weight[0]
    gradient = gradient_rows(tokens[0], master.astype(jnp.bfloat16), snapshot[0], n, blocks)
    first_new = BETA_ONE * moment_one[0] + (1.0 - BETA_ONE) * gradient
    second_new = BETA_TWO * moment_two[0] + (1.0 - BETA_TWO) * gradient * gradient
    step_dir = (
        first_new
        / (1.0 - BETA_ONE**STEP)
        / (jnp.sqrt(second_new / (1.0 - BETA_TWO**STEP)) + EPSILON)
    )
    updated = master - LEARN_RATE * (step_dir + DECAY * master)
    return (updated[None], first_new[None], second_new[None])


def solution(mesh):
    spec = P("blk", "fsdp", None)
    return jax.shard_map(
        functools.partial(per_device, mesh.shape["fsdp"], mesh.shape["blk"]),
        mesh=mesh,
        in_specs=(spec,) * 5,
        out_specs=(spec,) * 3,
        check_vma=False,
    )
```

```python
import functools
import math

import jax
import jax.numpy as jnp
from jax import lax
from jax.experimental import pallas as pl
from jax.experimental.pallas import tpu as pltpu
from jax.sharding import PartitionSpec as P

HEADS = 16
KVH = 4
HD = 128
SEQ = 256
STEP = 100
GROUP = HEADS // KVH
HEAD_ROWS = (GROUP + 1) * HD
UNITS = GROUP + 1

THETA = 500000.0
BETA_ONE = 0.9
BETA_TWO = 0.95
LEARN_RATE = 0.002
DECAY = 0.1
EPSILON = 1e-08
MASKED = -1e30
MESH = pl.DeviceIdType.MESH


def rotary_tables():
    positions = jnp.arange(SEQ).astype(jnp.float32)
    exponents = jnp.arange(HD // 2).astype(jnp.float32) * (2.0 / HD)
    angles = positions[:, None] * (THETA ** (-exponents))[None, :]
    cosine, sine = jnp.cos(angles), jnp.sin(angles)
    return (
        jnp.concatenate([cosine, cosine], axis=1),
        jnp.concatenate([-sine, sine], axis=1),
    )


def sequence_grad(x, w_student, w_teacher, cosine, sine):
    inv_root = 1.0 / math.sqrt(HD)

    def project(weight):
        raw = lax.dot_general(
            x, weight, (((1,), (1,)), ((), ())), preferred_element_type=jnp.float32
        )
        parts = []
        for head in range(GROUP + 1):
            part = raw[:, head * HD : (head + 1) * HD]
            turned = part * cosine + pltpu.roll(part, HD // 2, 1) * sine
            parts.append(turned.astype(jnp.bfloat16))
        return parts

    student, teacher = project(w_student), project(w_teacher)
    rows = lax.broadcasted_iota(jnp.int32, (SEQ, SEQ), 0)
    columns = lax.broadcasted_iota(jnp.int32, (SEQ, SEQ), 1)
    causal = rows >= columns

    def probs(query, key):
        scores = (
            lax.dot_general(
                query, key, (((1,), (1,)), ((), ())), preferred_element_type=jnp.float32
            )
            * inv_root
        )
        scores = jnp.where(causal, scores, MASKED)
        spread = jnp.exp(scores - jnp.max(scores, axis=-1, keepdims=True))
        return spread * (1.0 / jnp.sum(spread, axis=-1, keepdims=True))

    def turn_back(part):
        return (part * cosine - pltpu.roll(part, HD // 2, 1) * sine).astype(jnp.bfloat16)

    pieces = []
    key_grad = jnp.zeros((SEQ, HD), jnp.float32)
    for head in range(GROUP):
        spread = probs(student[head], student[GROUP]) - probs(teacher[head], teacher[GROUP])
        rounded = (jnp.where(causal, spread, 0.0) * (1.0 / HEADS)).astype(jnp.bfloat16)
        query_grad = jnp.dot(rounded, student[GROUP], preferred_element_type=jnp.float32)
        pieces.append(turn_back(query_grad * inv_root))
        key_grad += lax.dot_general(
            rounded, student[head], (((0,), (0,)), ((), ())), preferred_element_type=jnp.float32
        )
    pieces.append(turn_back(key_grad * inv_root))
    return jnp.concatenate(pieces, axis=1)


def kernel(
    n, blocks, seqs,
    tokens, student, teacher, cos_ref, sin_ref, out,
    held, weight, total, partial, extra,
    w_send, w_recv, s_send, s_recv, t_send, t_recv, g_send, g_recv, f_send, f_recv,
):
    share = n // KVH
    me, blk = lax.axis_index("fsdp"), lax.axis_index("blk")
    chip, lane = lax.div(me, share), lax.rem(me, share)
    last, helper, split = KVH - 1, KVH - 2, KVH - 2

    def placed(native):
        is_key = lax.div(native, HEADS * share)
        key = (native - HEADS * share) * is_key
        head = (1 - is_key) * lax.div(native, GROUP * share) + is_key * lax.div(key, share)
        at = (1 - is_key) * lax.rem(native, GROUP * share) + is_key * (
            GROUP * share + lax.rem(key, share)
        )
        return head * (UNITS * share) + at

    def native_of(place):
        head, at = lax.div(place, UNITS * share), lax.rem(place, UNITS * share)
        is_key = lax.div(at, GROUP * share)
        return (1 - is_key) * (GROUP * share * head + at) + is_key * (
            HEADS * share + share * head + at - GROUP * share
        )

    def each(count, body):
        def run(step, carry):
            body(step)
            return carry

        lax.fori_loop(0, count, run, 0)

    def landed(ref, sem):
        pltpu.make_async_copy(ref, ref, sem).wait()

    def to(src, dst, send_sem, recv_sem, device, group=None):
        target = {"fsdp": device, "blk": blk if group is None else group}
        return pltpu.make_async_remote_copy(
            src_ref=src, dst_ref=dst, send_sem=send_sem, recv_sem=recv_sem,
            device_id=target, device_id_type=MESH,
        )

    for seq in range(seqs):
        pltpu.make_async_copy(tokens.at[seq], held.at[chip, seq], t_recv.at[chip, seq]).start()

    barrier = pltpu.get_barrier_semaphore()
    after = lax.rem(blk + 1, blocks)
    before = lax.rem(blk + blocks - 1, blocks)

    def greet(step):
        pl.semaphore_signal(
            barrier, inc=1, device_id={"fsdp": lax.rem(me + 1 + step, n), "blk": blk},
            device_id_type=MESH,
        )

    def greet_teacher(step):
        pl.semaphore_signal(
            barrier, inc=1, device_id={"fsdp": step, "blk": before}, device_id_type=MESH
        )

    each(n - 1, greet)
    each(n, greet_teacher)
    pl.semaphore_wait(barrier, 2 * n - 1)

    def send_rows(unit):
        place = placed(me * UNITS + unit)
        owner, slot = lax.div(place, UNITS), lax.rem(place, UNITS)
        at = lax.rem(place, UNITS * share)

        def send(role, device):
            @pl.when(device == me)
            def _():
                pltpu.make_async_copy(
                    student.at[unit], weight.at[role, 0, at], w_recv.at[role, 0, slot]
                ).start()

            @pl.when(device != me)
            def _():
                to(
                    student.at[unit], weight.at[role, 0, at], w_send.at[role, 0, unit],
                    w_recv.at[role, 0, slot], device,
                ).start()

            to(
                teacher.at[unit], weight.at[role, 1, at], w_send.at[role, 1, unit],
                w_recv.at[role, 1, slot], device, after,
            ).start()

        send(0, owner)

        @pl.when(owner >= last * share)
        def _():
            send(1, owner - share)

    each(UNITS, send_rows)

    def pass_right(src, slot, seq):
        return to(src, held.at[slot, seq], t_send.at[0, slot, seq], t_recv.at[slot, seq], me + share)

    def pass_left(src, slot, seq):
        return to(src, held.at[slot, seq], t_send.at[1, slot, seq], t_recv.at[slot, seq], me - share)

    for seq in range(seqs):

        @pl.when(chip < KVH - 1)
        def _():
            pass_right(tokens.at[seq], chip, seq).start()

        @pl.when(chip > 0)
        def _():
            pass_left(tokens.at[seq], chip, seq).start()

    total[...] = jnp.zeros_like(total)

    def sibling(step):
        return chip * share + lax.rem(lane + step, share)

    def share_rows(role, which):
        def arrived(unit):
            landed(weight.at[role, which, lane * UNITS + unit], w_recv.at[role, which, unit])

        each(UNITS, arrived)
        mine = weight.at[role, which, pl.ds(lane * UNITS, UNITS)]
        for step in range(1, share):
            to(
                mine, mine, s_send.at[role, which, step - 1], s_recv.at[role, which, step - 1],
                sibling(step),
            ).start()

    def shared_rows(role, which):
        for step in range(1, share):
            lane_from = lax.rem(lane + share - step, share)
            landed(
                weight.at[role, which, pl.ds(lane_from * UNITS, UNITS)],
                s_recv.at[role, which, step - 1],
            )

    def each_role(body):
        body(0)

        @pl.when(chip == helper)
        def _():
            body(1)

    for which in range(2):
        each_role(functools.partial(share_rows, which=which))
    for which in range(2):
        each_role(functools.partial(shared_rows, which=which))

    def work(step):
        seq = lax.rem(step, seqs)
        distance = lax.div(step, 2 * seqs)
        side = lax.rem(lax.div(step, seqs), 2)
        slot = chip - distance + 2 * distance * side
        valid = (distance + 1 - side > 0) & (slot >= 0) & (slot < KVH)

        @pl.when(valid & ((chip < last) | (slot >= split)))
        def _():
            landed(held.at[slot, seq], t_recv.at[slot, seq])

            @pl.when((distance > 0) & (side == 0) & (chip < helper))
            def _():
                pass_right(held.at[slot, seq], slot, seq).start()

            @pl.when((distance > 0) & (side == 1) & (chip > 0))
            def _():
                pass_left(held.at[slot, seq], slot, seq).start()

            def add_gradient(role):
                x = held[slot, seq]
                grad = sequence_grad(
                    x,
                    weight[role, 0].reshape(HEAD_ROWS, -1),
                    weight[role, 1].reshape(HEAD_ROWS, -1),
                    cos_ref[...],
                    sin_ref[...],
                )
                width = 512
                for start in range(0, x.shape[1], width):
                    piece = lax.dot_general(
                        grad, x[:, start : start + width], (((0,), (0,)), ((), ())),
                        preferred_element_type=jnp.float32,
                    )
                    total[role, :, :, start : start + width] += piece.reshape(
                        UNITS * share, -1, width
                    )

            roles = 1 + lax.div(chip, helper) * lax.div(KVH - 1 - slot, split) * (last - chip)
            each(roles, add_gradient)

    each(2 * KVH * seqs, work)

    def send_partials(role):
        def send_partial(unit):
            for step in range(1, share):
                lane_to = lax.rem(lane + step, share)
                to(
                    total.at[role, lane_to * UNITS + unit], partial.at[role, step - 1, unit],
                    g_send.at[role, step - 1, unit], g_recv.at[role, step - 1, unit],
                    sibling(step),
                ).start()

        each(UNITS, send_partial)

    def send_sums(role):
        landing = (out, extra)[role]

        def send_sum(unit):
            at = lane * UNITS + unit
            native = native_of((me + role * share) * UNITS + unit)
            device, slot = lax.div(native, UNITS), lax.rem(native, UNITS)
            for step in range(1, share):
                landed(partial.at[role, step - 1, unit], g_recv.at[role, step - 1, unit])
                total[role, at] += partial[role, step - 1, unit]

            @pl.when(device == me)
            def _():
                pltpu.make_async_copy(
                    total.at[role, at], landing.at[slot], f_recv.at[role, slot]
                ).start()

            @pl.when(device != me)
            def _():
                to(
                    total.at[role, at], landing.at[slot], f_send.at[role, unit],
                    f_recv.at[role, slot], device,
                ).start()

        each(UNITS, send_sum)

    each_role(send_partials)
    each_role(send_sums)

    def arrive(unit):
        landed(out.at[unit], f_recv.at[0, unit])

        @pl.when(placed(me * UNITS + unit) >= last * share * UNITS)
        def _():
            landed(extra.at[unit], f_recv.at[1, unit])
            out[unit] += extra[unit]

    each(UNITS, arrive)

    def sent(unit):
        owner = lax.div(placed(me * UNITS + unit), UNITS)

        def rows_left(role, device):
            @pl.when(device != me)
            def _():
                landed(student.at[unit], w_send.at[role, 0, unit])

            landed(teacher.at[unit], w_send.at[role, 1, unit])

        rows_left(0, owner)

        @pl.when(owner >= last * share)
        def _():
            rows_left(1, owner - share)

        def sums_left(role):
            for step in range(1, share):
                landed(partial.at[role, step - 1, unit], g_send.at[role, step - 1, unit])

            @pl.when(lax.div(native_of((me + role * share) * UNITS + unit), UNITS) != me)
            def _():
                landed(out.at[unit], f_send.at[role, unit])

        each_role(sums_left)

    each(UNITS, sent)

    def shares_left(role):
        for which in range(2):
            for step in range(1, share):
                landed(
                    weight.at[role, which, pl.ds(lane * UNITS, UNITS)],
                    s_send.at[role, which, step - 1],
                )

    each_role(shares_left)

    def sent_tokens(step):
        slot, seq = lax.div(step, seqs), lax.rem(step, seqs)

        @pl.when((slot <= chip) & ((chip < helper) | ((chip == helper) & (slot == chip))))
        def _():
            landed(held.at[slot, seq], t_send.at[0, slot, seq])

        @pl.when((slot >= chip) & (chip > 0))
        def _():
            landed(held.at[slot, seq], t_send.at[1, slot, seq])

    each(KVH * seqs, sent_tokens)


def gradient_rows(tokens, student_copy, snapshot, n, blocks):
    rows, width = student_copy.shape
    seqs = tokens.shape[0] // SEQ
    share = n // KVH
    unit = rows // UNITS
    cosine, sine = rotary_tables()
    dma = pltpu.SemaphoreType.DMA
    anywhere, vmem = pl.BlockSpec(memory_space=pl.ANY), pl.BlockSpec(memory_space=pltpu.VMEM)
    gradient = pl.pallas_call(
        functools.partial(kernel, n, blocks, seqs),
        out_shape=jax.ShapeDtypeStruct((UNITS, unit, width), jnp.float32),
        in_specs=[anywhere, anywhere, anywhere, vmem, vmem],
        out_specs=vmem,
        scratch_shapes=[
            pltpu.VMEM((KVH, seqs, SEQ, width), jnp.bfloat16),
            pltpu.VMEM((2, 2, UNITS * share, unit, width), jnp.bfloat16),
            pltpu.VMEM((2, UNITS * share, unit, width), jnp.float32),
            pltpu.VMEM((2, share - 1, UNITS, unit, width), jnp.float32),
            pltpu.VMEM((UNITS, unit, width), jnp.float32),
            dma((2, 2, UNITS)),
            dma((2, 2, UNITS)),
            dma((2, 2, share - 1)),
            dma((2, 2, share - 1)),
            dma((2, KVH, seqs)),
            dma((KVH, seqs)),
            dma((2, share - 1, UNITS)),
            dma((2, share - 1, UNITS)),
            dma((2, UNITS)),
            dma((2, UNITS)),
        ],
        compiler_params=pltpu.CompilerParams(
            collective_id=0, has_side_effects=True, vmem_limit_bytes=56 * 1024 * 1024
        ),
    )(
        tokens.reshape(seqs, SEQ, width),
        student_copy.reshape(UNITS, unit, width),
        snapshot.reshape(UNITS, unit, width),
        cosine,
        sine,
    )
    return gradient.reshape(rows, width)


def per_device(n, blocks, tokens, student_weight, snapshot, moment_one, moment_two):
    master = student_weight[0]
    gradient = gradient_rows(tokens[0], master.astype(jnp.bfloat16), snapshot[0], n, blocks)
    first_new = BETA_ONE * moment_one[0] + (1.0 - BETA_ONE) * gradient
    second_new = BETA_TWO * moment_two[0] + (1.0 - BETA_TWO) * gradient * gradient
    step_dir = (
        first_new
        / (1.0 - BETA_ONE**STEP)
        / (jnp.sqrt(second_new / (1.0 - BETA_TWO**STEP)) + EPSILON)
    )
    updated = master - LEARN_RATE * (step_dir + DECAY * master)
    return (updated[None], first_new[None], second_new[None])


def solution(mesh):
    spec = P("blk", "fsdp", None)
    return jax.shard_map(
        functools.partial(per_device, mesh.shape["fsdp"], mesh.shape["blk"]),
        mesh=mesh,
        in_specs=(spec,) * 5,
        out_specs=(spec,) * 3,
        check_vma=False,
    )
```

```python
import functools
import math

import jax
import jax.numpy as jnp
from jax import lax
from jax.experimental import pallas as pl
from jax.experimental.pallas import tpu as pltpu
from jax.sharding import PartitionSpec as P

HEADS = 16
KVH = 4
HD = 128
SEQ = 256
STEP = 100
GROUP = HEADS // KVH
HEAD_ROWS = (GROUP + 1) * HD
UNITS = GROUP + 1

THETA = 500000.0
BETA_ONE = 0.9
BETA_TWO = 0.95
LEARN_RATE = 0.002
DECAY = 0.1
EPSILON = 1e-08
MASKED = -1e30
MESH = pl.DeviceIdType.MESH


def rotary_tables():
    positions = jnp.arange(SEQ).astype(jnp.float32)
    exponents = jnp.arange(HD // 2).astype(jnp.float32) * (2.0 / HD)
    angles = positions[:, None] * (THETA ** (-exponents))[None, :]
    cosine, sine = jnp.cos(angles), jnp.sin(angles)
    return (
        jnp.concatenate([cosine, cosine], axis=1),
        jnp.concatenate([-sine, sine], axis=1),
    )


def sequence_grad(x, w_student, w_teacher, cosine, sine):
    inv_root = 1.0 / math.sqrt(HD)

    def project(weight):
        raw = lax.dot_general(
            x, weight, (((1,), (1,)), ((), ())), preferred_element_type=jnp.float32
        )
        parts = []
        for head in range(GROUP + 1):
            part = raw[:, head * HD : (head + 1) * HD]
            turned = part * cosine + pltpu.roll(part, HD // 2, 1) * sine
            parts.append(turned.astype(jnp.bfloat16))
        return parts

    student, teacher = project(w_student), project(w_teacher)
    rows = lax.broadcasted_iota(jnp.int32, (SEQ, SEQ), 0)
    columns = lax.broadcasted_iota(jnp.int32, (SEQ, SEQ), 1)
    causal = rows >= columns

    def probs(query, key):
        scores = (
            lax.dot_general(
                query, key, (((1,), (1,)), ((), ())), preferred_element_type=jnp.float32
            )
            * inv_root
        )
        scores = jnp.where(causal, scores, MASKED)
        spread = jnp.exp(scores - jnp.max(scores, axis=-1, keepdims=True))
        return spread * (1.0 / jnp.sum(spread, axis=-1, keepdims=True))

    def turn_back(part):
        return (part * cosine - pltpu.roll(part, HD // 2, 1) * sine).astype(jnp.bfloat16)

    pieces = []
    key_grad = jnp.zeros((SEQ, HD), jnp.float32)
    for head in range(GROUP):
        spread = probs(student[head], student[GROUP]) - probs(teacher[head], teacher[GROUP])
        rounded = (jnp.where(causal, spread, 0.0) * (1.0 / HEADS)).astype(jnp.bfloat16)
        query_grad = jnp.dot(rounded, student[GROUP], preferred_element_type=jnp.float32)
        pieces.append(turn_back(query_grad * inv_root))
        key_grad += lax.dot_general(
            rounded, student[head], (((0,), (0,)), ((), ())), preferred_element_type=jnp.float32
        )
    pieces.append(turn_back(key_grad * inv_root))
    return jnp.concatenate(pieces, axis=1)


def kernel(
    n, blocks, seqs,
    tokens, student, teacher, cos_ref, sin_ref, out,
    held, weight, total, partial, extra,
    w_send, w_recv, s_send, s_recv, t_send, t_recv, g_send, g_recv, f_send, f_recv,
):
    share = n // KVH
    me, blk = lax.axis_index("fsdp"), lax.axis_index("blk")
    chip, lane = lax.div(me, share), lax.rem(me, share)
    last, helper, split = KVH - 1, KVH - 2, KVH - 2

    def placed(native):
        is_key = lax.div(native, HEADS * share)
        key = (native - HEADS * share) * is_key
        head = (1 - is_key) * lax.div(native, GROUP * share) + is_key * lax.div(key, share)
        at = (1 - is_key) * lax.rem(native, GROUP * share) + is_key * (
            GROUP * share + lax.rem(key, share)
        )
        return head * (UNITS * share) + at

    def native_of(place):
        head, at = lax.div(place, UNITS * share), lax.rem(place, UNITS * share)
        is_key = lax.div(at, GROUP * share)
        return (1 - is_key) * (GROUP * share * head + at) + is_key * (
            HEADS * share + share * head + at - GROUP * share
        )

    def each(count, body):
        def run(step, carry):
            body(step)
            return carry

        lax.fori_loop(0, count, run, 0)

    def landed(ref, sem):
        pltpu.make_async_copy(ref, ref, sem).wait()

    def to(src, dst, send_sem, recv_sem, device, group=None):
        target = {"fsdp": device, "blk": blk if group is None else group}
        return pltpu.make_async_remote_copy(
            src_ref=src, dst_ref=dst, send_sem=send_sem, recv_sem=recv_sem,
            device_id=target, device_id_type=MESH,
        )

    for seq in range(seqs):
        pltpu.make_async_copy(tokens.at[seq], held.at[chip, seq], t_recv.at[chip, seq]).start()

    barrier = pltpu.get_barrier_semaphore()
    after = lax.rem(blk + 1, blocks)
    before = lax.rem(blk + blocks - 1, blocks)

    def greet(step):
        pl.semaphore_signal(
            barrier, inc=1, device_id={"fsdp": lax.rem(me + 1 + step, n), "blk": blk},
            device_id_type=MESH,
        )

    def greet_teacher(step):
        pl.semaphore_signal(
            barrier, inc=1, device_id={"fsdp": step, "blk": before}, device_id_type=MESH
        )

    each(n - 1, greet)
    each(n, greet_teacher)
    pl.semaphore_wait(barrier, 2 * n - 1)

    def send_rows(unit, role):
        place = placed(me * UNITS + unit)
        owner, slot = lax.div(place, UNITS), lax.rem(place, UNITS)
        at = lax.rem(place, UNITS * share)

        def send(device):
            @pl.when(device == me)
            def _():
                pltpu.make_async_copy(
                    student.at[unit], weight.at[role, 0, at], w_recv.at[role, 0, slot]
                ).start()

            @pl.when(device != me)
            def _():
                to(
                    student.at[unit], weight.at[role, 0, at], w_send.at[role, 0, unit],
                    w_recv.at[role, 0, slot], device,
                ).start()

            to(
                teacher.at[unit], weight.at[role, 1, at], w_send.at[role, 1, unit],
                w_recv.at[role, 1, slot], device, after,
            ).start()

        if role == 0:
            send(owner)
        else:

            @pl.when(owner >= last * share)
            def _():
                send(owner - share)

    each(UNITS, functools.partial(send_rows, role=0))

    @pl.when(chip < last)
    def _():
        each(UNITS, functools.partial(send_rows, role=1))

    def pass_right(src, slot, seq):
        return to(src, held.at[slot, seq], t_send.at[0, slot, seq], t_recv.at[slot, seq], me + share)

    def pass_left(src, slot, seq):
        return to(src, held.at[slot, seq], t_send.at[1, slot, seq], t_recv.at[slot, seq], me - share)

    for seq in range(seqs):

        @pl.when(chip < KVH - 1)
        def _():
            pass_right(tokens.at[seq], chip, seq).start()

        @pl.when(chip > 0)
        def _():
            pass_left(tokens.at[seq], chip, seq).start()

    total[...] = jnp.zeros_like(total)

    def sibling(step):
        return chip * share + lax.rem(lane + step, share)

    def share_rows(role, which):
        def arrived(unit):
            landed(weight.at[role, which, lane * UNITS + unit], w_recv.at[role, which, unit])

        each(UNITS, arrived)
        mine = weight.at[role, which, pl.ds(lane * UNITS, UNITS)]
        for step in range(1, share):
            to(
                mine, mine, s_send.at[role, which, step - 1], s_recv.at[role, which, step - 1],
                sibling(step),
            ).start()

    def shared_rows(role, which):
        for step in range(1, share):
            lane_from = lax.rem(lane + share - step, share)
            landed(
                weight.at[role, which, pl.ds(lane_from * UNITS, UNITS)],
                s_recv.at[role, which, step - 1],
            )

    def each_role(body):
        body(0)

        @pl.when(chip == helper)
        def _():
            body(1)

    @pl.when(chip == last)
    def _():
        for seq in range(seqs):
            landed(held.at[chip, seq], t_send.at[1, chip, seq])
        each(UNITS, functools.partial(send_rows, role=1))

    for which in range(2):
        share_rows(0, which)
    for which in range(2):
        shared_rows(0, which)

    def chunk(step):
        turn, seq = lax.div(step, seqs), lax.rem(step, seqs)
        distance, side = lax.div(turn + 1, 2), lax.rem(turn, 2)
        slot = chip - distance + 2 * distance * side
        valid = (slot >= 0) & (slot < KVH) & ((chip < last) | (slot >= split))
        relayed = valid & (
            ((side == 1) & (chip > 0)) | ((side == 0) & (distance > 0) & (chip < helper))
        )
        return slot, seq, side, valid, relayed

    def relay(step):
        slot, seq, side, _, relayed = chunk(step)

        @pl.when(relayed)
        def _():
            landed(held.at[slot, seq], t_recv.at[slot, seq])

            @pl.when(side == 0)
            def _():
                pass_right(held.at[slot, seq], slot, seq).start()

            @pl.when(side == 1)
            def _():
                pass_left(held.at[slot, seq], slot, seq).start()

    def work(step):
        relay(step + seqs)
        slot, seq, side, valid, relayed = chunk(step)

        @pl.when((step == 2 * seqs) & (chip == helper))
        def _():
            for which in range(2):
                share_rows(1, which)
            for which in range(2):
                shared_rows(1, which)

        @pl.when(valid)
        def _():
            @pl.when(jnp.logical_not(relayed))
            def _():
                landed(held.at[slot, seq], t_recv.at[slot, seq])

            def add_gradient(role):
                x = held[slot, seq]
                grad = sequence_grad(
                    x,
                    weight[role, 0].reshape(HEAD_ROWS, -1),
                    weight[role, 1].reshape(HEAD_ROWS, -1),
                    cos_ref[...],
                    sin_ref[...],
                )
                width = 512
                for start in range(0, x.shape[1], width):
                    piece = lax.dot_general(
                        grad, x[:, start : start + width], (((0,), (0,)), ((), ())),
                        preferred_element_type=jnp.float32,
                    )
                    total[role, :, :, start : start + width] += piece.reshape(
                        UNITS * share, -1, width
                    )

            roles = 1 + lax.div(chip, helper) * lax.div(KVH - 1 - slot, split) * (last - chip)
            each(roles, add_gradient)

    each((2 * KVH - 1) * seqs, work)

    def send_partials(role):
        def send_partial(step):
            unit = UNITS - 1 - step
            for hop in range(1, share):
                lane_to = lax.rem(lane + hop, share)
                to(
                    total.at[role, lane_to * UNITS + unit], partial.at[role, hop - 1, unit],
                    g_send.at[role, hop - 1, unit], g_recv.at[role, hop - 1, unit],
                    sibling(hop),
                ).start()

        each(UNITS, send_partial)

    def send_sums(role):
        landing = (out, extra)[role]

        def send_sum(step):
            unit = UNITS - 1 - step
            at = lane * UNITS + unit
            native = native_of((me + role * share) * UNITS + unit)
            device, slot = lax.div(native, UNITS), lax.rem(native, UNITS)
            for hop in range(1, share):
                landed(partial.at[role, hop - 1, unit], g_recv.at[role, hop - 1, unit])
                total[role, at] += partial[role, hop - 1, unit]

            @pl.when(device == me)
            def _():
                pltpu.make_async_copy(
                    total.at[role, at], landing.at[slot], f_recv.at[role, slot]
                ).start()

            @pl.when(device != me)
            def _():
                to(
                    total.at[role, at], landing.at[slot], f_send.at[role, unit],
                    f_recv.at[role, slot], device,
                ).start()

        each(UNITS, send_sum)

    each_role(send_partials)
    each_role(send_sums)

    def arrive(unit):
        landed(out.at[unit], f_recv.at[0, unit])

        @pl.when(placed(me * UNITS + unit) >= last * share * UNITS)
        def _():
            landed(extra.at[unit], f_recv.at[1, unit])
            out[unit] += extra[unit]

    each(UNITS, arrive)

    def sent(unit):
        owner = lax.div(placed(me * UNITS + unit), UNITS)

        def rows_left(role, device):
            @pl.when(device != me)
            def _():
                landed(student.at[unit], w_send.at[role, 0, unit])

            landed(teacher.at[unit], w_send.at[role, 1, unit])

        rows_left(0, owner)

        @pl.when(owner >= last * share)
        def _():
            rows_left(1, owner - share)

        def sums_left(role):
            for step in range(1, share):
                landed(partial.at[role, step - 1, unit], g_send.at[role, step - 1, unit])

            @pl.when(lax.div(native_of((me + role * share) * UNITS + unit), UNITS) != me)
            def _():
                landed(out.at[unit], f_send.at[role, unit])

        each_role(sums_left)

    each(UNITS, sent)

    def shares_left(role):
        for which in range(2):
            for step in range(1, share):
                landed(
                    weight.at[role, which, pl.ds(lane * UNITS, UNITS)],
                    s_send.at[role, which, step - 1],
                )

    each_role(shares_left)

    def sent_tokens(step):
        slot, seq = lax.div(step, seqs), lax.rem(step, seqs)

        @pl.when((slot <= chip) & ((chip < helper) | ((chip == helper) & (slot == chip))))
        def _():
            landed(held.at[slot, seq], t_send.at[0, slot, seq])

        @pl.when((slot >= chip) & (chip > 0) & (chip < last))
        def _():
            landed(held.at[slot, seq], t_send.at[1, slot, seq])

    each(KVH * seqs, sent_tokens)


def gradient_rows(tokens, student_copy, snapshot, n, blocks):
    rows, width = student_copy.shape
    seqs = tokens.shape[0] // SEQ
    share = n // KVH
    unit = rows // UNITS
    cosine, sine = rotary_tables()
    dma = pltpu.SemaphoreType.DMA
    anywhere, vmem = pl.BlockSpec(memory_space=pl.ANY), pl.BlockSpec(memory_space=pltpu.VMEM)
    gradient = pl.pallas_call(
        functools.partial(kernel, n, blocks, seqs),
        out_shape=jax.ShapeDtypeStruct((UNITS, unit, width), jnp.float32),
        in_specs=[anywhere, anywhere, anywhere, vmem, vmem],
        out_specs=vmem,
        scratch_shapes=[
            pltpu.VMEM((KVH, seqs, SEQ, width), jnp.bfloat16),
            pltpu.VMEM((2, 2, UNITS * share, unit, width), jnp.bfloat16),
            pltpu.VMEM((2, UNITS * share, unit, width), jnp.float32),
            pltpu.VMEM((2, share - 1, UNITS, unit, width), jnp.float32),
            pltpu.VMEM((UNITS, unit, width), jnp.float32),
            dma((2, 2, UNITS)),
            dma((2, 2, UNITS)),
            dma((2, 2, share - 1)),
            dma((2, 2, share - 1)),
            dma((2, KVH, seqs)),
            dma((KVH, seqs)),
            dma((2, share - 1, UNITS)),
            dma((2, share - 1, UNITS)),
            dma((2, UNITS)),
            dma((2, UNITS)),
        ],
        compiler_params=pltpu.CompilerParams(
            collective_id=0, has_side_effects=True, vmem_limit_bytes=56 * 1024 * 1024
        ),
    )(
        tokens.reshape(seqs, SEQ, width),
        student_copy.reshape(UNITS, unit, width),
        snapshot.reshape(UNITS, unit, width),
        cosine,
        sine,
    )
    return gradient.reshape(rows, width)


def per_device(n, blocks, tokens, student_weight, snapshot, moment_one, moment_two):
    master = student_weight[0]
    gradient = gradient_rows(tokens[0], master.astype(jnp.bfloat16), snapshot[0], n, blocks)
    first_new = BETA_ONE * moment_one[0] + (1.0 - BETA_ONE) * gradient
    second_new = BETA_TWO * moment_two[0] + (1.0 - BETA_TWO) * gradient * gradient
    step_dir = (
        first_new
        / (1.0 - BETA_ONE**STEP)
        / (jnp.sqrt(second_new / (1.0 - BETA_TWO**STEP)) + EPSILON)
    )
    updated = master - LEARN_RATE * (step_dir + DECAY * master)
    return (updated[None], first_new[None], second_new[None])


def solution(mesh):
    spec = P("blk", "fsdp", None)
    return jax.shard_map(
        functools.partial(per_device, mesh.shape["fsdp"], mesh.shape["blk"]),
        mesh=mesh,
        in_specs=(spec,) * 5,
        out_specs=(spec,) * 3,
        check_vma=False,
    )
```

```python
import functools
import math

import jax
import jax.numpy as jnp
from jax import lax
from jax.experimental import pallas as pl
from jax.experimental.pallas import tpu as pltpu
from jax.sharding import PartitionSpec as P

HEADS = 16
KVH = 4
HD = 128
SEQ = 256
STEP = 100
GROUP = HEADS // KVH
HEAD_ROWS = (GROUP + 1) * HD
UNITS = GROUP + 1

THETA = 500000.0
BETA_ONE = 0.9
BETA_TWO = 0.95
LEARN_RATE = 0.002
DECAY = 0.1
EPSILON = 1e-08
MASKED = -1e30
MESH = pl.DeviceIdType.MESH


def rotary_tables():
    positions = jnp.arange(SEQ).astype(jnp.float32)
    exponents = jnp.arange(HD // 2).astype(jnp.float32) * (2.0 / HD)
    angles = positions[:, None] * (THETA ** (-exponents))[None, :]
    cosine, sine = jnp.cos(angles), jnp.sin(angles)
    return (
        jnp.concatenate([cosine, cosine], axis=1),
        jnp.concatenate([-sine, sine], axis=1),
    )


def group_grad(x, w_student, w_teacher, cosine, sine):
    inv_root = 1.0 / math.sqrt(HD)

    def project(weight):
        return lax.dot_general(
            x, weight, (((1,), (1,)), ((), ())), preferred_element_type=jnp.float32
        )

    def heads_of(raw):
        parts = []
        for head in range(GROUP + 1):
            part = raw[:, head * HD : (head + 1) * HD]
            turned = part * cosine + pltpu.roll(part, HD // 2, 1) * sine
            parts.append(turned.astype(jnp.bfloat16))
        return parts

    raw_student, raw_teacher = project(w_student), project(w_teacher)
    rows = lax.broadcasted_iota(jnp.int32, (SEQ, SEQ), 0)
    columns = lax.broadcasted_iota(jnp.int32, (SEQ, SEQ), 1)
    causal = rows >= columns

    def probs(query, key):
        scores = (
            lax.dot_general(
                query, key, (((1,), (1,)), ((), ())), preferred_element_type=jnp.float32
            )
            * inv_root
        )
        scores = jnp.where(causal, scores, MASKED)
        spread = jnp.exp(scores - jnp.max(scores, axis=-1, keepdims=True))
        return spread * (1.0 / jnp.sum(spread, axis=-1, keepdims=True))

    def turn_back(part):
        return (part * cosine - pltpu.roll(part, HD // 2, 1) * sine).astype(jnp.bfloat16)

    results = []
    for start in range(0, x.shape[0], SEQ):
        student = heads_of(raw_student[start : start + SEQ])
        teacher = heads_of(raw_teacher[start : start + SEQ])
        pieces = []
        key_grad = jnp.zeros((SEQ, HD), jnp.float32)
        for head in range(GROUP):
            spread = probs(student[head], student[GROUP]) - probs(teacher[head], teacher[GROUP])
            rounded = (jnp.where(causal, spread, 0.0) * (1.0 / HEADS)).astype(jnp.bfloat16)
            query_grad = jnp.dot(rounded, student[GROUP], preferred_element_type=jnp.float32)
            pieces.append(turn_back(query_grad * inv_root))
            key_grad += lax.dot_general(
                rounded, student[head], (((0,), (0,)), ((), ())),
                preferred_element_type=jnp.float32,
            )
        pieces.append(turn_back(key_grad * inv_root))
        results.append(jnp.concatenate(pieces, axis=1))
    return jnp.concatenate(results, axis=0)


def kernel(
    n, blocks, seqs,
    tokens, student, teacher, cos_ref, sin_ref, out,
    held, weight, total, partial, extra,
    w_send, w_recv, s_send, s_recv, t_send, t_recv, g_send, g_recv, f_send, f_recv,
):
    share = n // KVH
    me, blk = lax.axis_index("fsdp"), lax.axis_index("blk")
    chip, lane = lax.div(me, share), lax.rem(me, share)
    last, helper, split = KVH - 1, KVH - 2, KVH - 2

    def placed(native):
        is_key = lax.div(native, HEADS * share)
        key = (native - HEADS * share) * is_key
        head = (1 - is_key) * lax.div(native, GROUP * share) + is_key * lax.div(key, share)
        at = (1 - is_key) * lax.rem(native, GROUP * share) + is_key * (
            GROUP * share + lax.rem(key, share)
        )
        return head * (UNITS * share) + at

    def native_of(place):
        head, at = lax.div(place, UNITS * share), lax.rem(place, UNITS * share)
        is_key = lax.div(at, GROUP * share)
        return (1 - is_key) * (GROUP * share * head + at) + is_key * (
            HEADS * share + share * head + at - GROUP * share
        )

    def each(count, body):
        def run(step, carry):
            body(step)
            return carry

        lax.fori_loop(0, count, run, 0)

    def landed(ref, sem):
        pltpu.make_async_copy(ref, ref, sem).wait()

    def to(src, dst, send_sem, recv_sem, device, group=None):
        target = {"fsdp": device, "blk": blk if group is None else group}
        return pltpu.make_async_remote_copy(
            src_ref=src, dst_ref=dst, send_sem=send_sem, recv_sem=recv_sem,
            device_id=target, device_id_type=MESH,
        )

    for seq in range(seqs):
        pltpu.make_async_copy(tokens.at[seq], held.at[chip, seq], t_recv.at[chip, seq]).start()

    barrier = pltpu.get_barrier_semaphore()
    after = lax.rem(blk + 1, blocks)
    before = lax.rem(blk + blocks - 1, blocks)

    def greet(step):
        pl.semaphore_signal(
            barrier, inc=1, device_id={"fsdp": lax.rem(me + 1 + step, n), "blk": blk},
            device_id_type=MESH,
        )

    def greet_teacher(step):
        pl.semaphore_signal(
            barrier, inc=1, device_id={"fsdp": step, "blk": before}, device_id_type=MESH
        )

    each(n - 1, greet)
    each(n, greet_teacher)
    pl.semaphore_wait(barrier, 2 * n - 1)

    def send_rows(unit, role):
        place = placed(me * UNITS + unit)
        owner, slot = lax.div(place, UNITS), lax.rem(place, UNITS)
        at = lax.rem(place, UNITS * share)

        def send(device):
            @pl.when(device == me)
            def _():
                pltpu.make_async_copy(
                    student.at[unit], weight.at[role, 0, at], w_recv.at[role, 0, slot]
                ).start()

            @pl.when(device != me)
            def _():
                to(
                    student.at[unit], weight.at[role, 0, at], w_send.at[role, 0, unit],
                    w_recv.at[role, 0, slot], device,
                ).start()

            to(
                teacher.at[unit], weight.at[role, 1, at], w_send.at[role, 1, unit],
                w_recv.at[role, 1, slot], device, after,
            ).start()

        if role == 0:
            send(owner)
        else:

            @pl.when(owner >= last * share)
            def _():
                send(owner - share)

    each(UNITS, functools.partial(send_rows, role=0))

    @pl.when(chip < last)
    def _():
        each(UNITS, functools.partial(send_rows, role=1))

    def pass_right(src, slot, seq):
        return to(src, held.at[slot, seq], t_send.at[0, slot, seq], t_recv.at[slot, seq], me + share)

    def pass_left(src, slot, seq):
        return to(src, held.at[slot, seq], t_send.at[1, slot, seq], t_recv.at[slot, seq], me - share)

    for seq in range(seqs):

        @pl.when(chip < KVH - 1)
        def _():
            pass_right(tokens.at[seq], chip, seq).start()

        @pl.when(chip > 0)
        def _():
            pass_left(tokens.at[seq], chip, seq).start()

    total[...] = jnp.zeros_like(total)

    def sibling(step):
        return chip * share + lax.rem(lane + step, share)

    def share_rows(role, which):
        def arrived(unit):
            landed(weight.at[role, which, lane * UNITS + unit], w_recv.at[role, which, unit])

        each(UNITS, arrived)
        mine = weight.at[role, which, pl.ds(lane * UNITS, UNITS)]
        for step in range(1, share):
            to(
                mine, mine, s_send.at[role, which, step - 1], s_recv.at[role, which, step - 1],
                sibling(step),
            ).start()

    def shared_rows(role, which):
        for step in range(1, share):
            lane_from = lax.rem(lane + share - step, share)
            landed(
                weight.at[role, which, pl.ds(lane_from * UNITS, UNITS)],
                s_recv.at[role, which, step - 1],
            )

    def each_role(body):
        body(0)

        @pl.when(chip == helper)
        def _():
            body(1)

    @pl.when(chip == last)
    def _():
        for seq in range(seqs):
            landed(held.at[chip, seq], t_send.at[1, chip, seq])
        each(UNITS, functools.partial(send_rows, role=1))

    for which in range(2):
        share_rows(0, which)
    for which in range(2):
        shared_rows(0, which)

    def send_partials(role):
        def send_partial(step):
            unit = UNITS - 1 - step
            for hop in range(1, share):
                lane_to = lax.rem(lane + hop, share)
                to(
                    total.at[role, lane_to * UNITS + unit], partial.at[role, hop - 1, unit],
                    g_send.at[role, hop - 1, unit], g_recv.at[role, hop - 1, unit],
                    sibling(hop),
                ).start()

        each(UNITS, send_partial)

    def send_sums(role):
        landing = (out, extra)[role]

        def send_sum(step):
            unit = UNITS - 1 - step
            at = lane * UNITS + unit
            native = native_of((me + role * share) * UNITS + unit)
            device, slot = lax.div(native, UNITS), lax.rem(native, UNITS)
            for hop in range(1, share):
                landed(partial.at[role, hop - 1, unit], g_recv.at[role, hop - 1, unit])
                total[role, at] += partial[role, hop - 1, unit]

            @pl.when(device == me)
            def _():
                pltpu.make_async_copy(
                    total.at[role, at], landing.at[slot], f_recv.at[role, slot]
                ).start()

            @pl.when(device != me)
            def _():
                to(
                    total.at[role, at], landing.at[slot], f_send.at[role, unit],
                    f_recv.at[role, slot], device,
                ).start()

        each(UNITS, send_sum)

    def chunk(turn):
        distance, side = lax.div(turn + 1, 2), lax.rem(turn, 2)
        slot = chip - distance + 2 * distance * side
        valid = (slot >= 0) & (slot < KVH) & ((chip < last) | (slot >= split))
        relayed = valid & (
            ((side == 1) & (chip > 0)) | ((side == 0) & (distance > 0) & (chip < helper))
        )
        return slot, side, valid, relayed

    def relay(turn):
        slot, side, _, relayed = chunk(turn)

        def relay_one(seq):
            landed(held.at[slot, seq], t_recv.at[slot, seq])

            @pl.when(side == 0)
            def _():
                pass_right(held.at[slot, seq], slot, seq).start()

            @pl.when(side == 1)
            def _():
                pass_left(held.at[slot, seq], slot, seq).start()

        @pl.when(relayed)
        def _():
            each(seqs, relay_one)

    def work(turn):
        @pl.when(turn >= 2)
        def _():
            relay(turn + 1)

        slot, _, valid, relayed = chunk(turn)

        @pl.when((turn == 2) & (chip == helper))
        def _():
            for which in range(2):
                share_rows(1, which)
            for which in range(2):
                shared_rows(1, which)

        @pl.when(valid)
        def _():
            @pl.when(jnp.logical_not(relayed))
            def _():
                each(seqs, lambda seq: landed(held.at[slot, seq], t_recv.at[slot, seq]))

            roles = 1 + lax.div(chip, helper) * lax.div(KVH - 1 - slot, split) * (last - chip)

            def add_gradient(step):
                role = roles - 1 - step
                x = held[slot].reshape(seqs * SEQ, -1)
                grad = group_grad(
                    x,
                    weight[role, 0].reshape(HEAD_ROWS, -1),
                    weight[role, 1].reshape(HEAD_ROWS, -1),
                    cos_ref[...],
                    sin_ref[...],
                )
                width = 512
                for start in range(0, x.shape[1], width):
                    piece = lax.dot_general(
                        grad, x[:, start : start + width], (((0,), (0,)), ((), ())),
                        preferred_element_type=jnp.float32,
                    )
                    total[role, :, :, start : start + width] += piece.reshape(
                        UNITS * share, -1, width
                    )

                @pl.when((role == 1) & (slot == 0))
                def _():
                    send_partials(1)
                    send_sums(1)

            each(roles, add_gradient)

    relay(2)
    relay(1)
    each(2 * KVH - 1, work)

    send_partials(0)
    send_sums(0)

    def arrive(unit):
        landed(out.at[unit], f_recv.at[0, unit])

        @pl.when(placed(me * UNITS + unit) >= last * share * UNITS)
        def _():
            landed(extra.at[unit], f_recv.at[1, unit])
            out[unit] += extra[unit]

    each(UNITS, arrive)

    def sent(unit):
        owner = lax.div(placed(me * UNITS + unit), UNITS)

        def rows_left(role, device):
            @pl.when(device != me)
            def _():
                landed(student.at[unit], w_send.at[role, 0, unit])

            landed(teacher.at[unit], w_send.at[role, 1, unit])

        rows_left(0, owner)

        @pl.when(owner >= last * share)
        def _():
            rows_left(1, owner - share)

        def sums_left(role):
            for step in range(1, share):
                landed(partial.at[role, step - 1, unit], g_send.at[role, step - 1, unit])

            @pl.when(lax.div(native_of((me + role * share) * UNITS + unit), UNITS) != me)
            def _():
                landed(out.at[unit], f_send.at[role, unit])

        each_role(sums_left)

    each(UNITS, sent)

    def shares_left(role):
        for which in range(2):
            for step in range(1, share):
                landed(
                    weight.at[role, which, pl.ds(lane * UNITS, UNITS)],
                    s_send.at[role, which, step - 1],
                )

    each_role(shares_left)

    def sent_tokens(step):
        slot, seq = lax.div(step, seqs), lax.rem(step, seqs)

        @pl.when((slot <= chip) & ((chip < helper) | ((chip == helper) & (slot == chip))))
        def _():
            landed(held.at[slot, seq], t_send.at[0, slot, seq])

        @pl.when((slot >= chip) & (chip > 0) & (chip < last))
        def _():
            landed(held.at[slot, seq], t_send.at[1, slot, seq])

    each(KVH * seqs, sent_tokens)


def gradient_rows(tokens, student_copy, snapshot, n, blocks):
    rows, width = student_copy.shape
    seqs = tokens.shape[0] // SEQ
    share = n // KVH
    unit = rows // UNITS
    cosine, sine = rotary_tables()
    dma = pltpu.SemaphoreType.DMA
    anywhere, vmem = pl.BlockSpec(memory_space=pl.ANY), pl.BlockSpec(memory_space=pltpu.VMEM)
    gradient = pl.pallas_call(
        functools.partial(kernel, n, blocks, seqs),
        out_shape=jax.ShapeDtypeStruct((UNITS, unit, width), jnp.float32),
        in_specs=[anywhere, anywhere, anywhere, vmem, vmem],
        out_specs=vmem,
        scratch_shapes=[
            pltpu.VMEM((KVH, seqs, SEQ, width), jnp.bfloat16),
            pltpu.VMEM((2, 2, UNITS * share, unit, width), jnp.bfloat16),
            pltpu.VMEM((2, UNITS * share, unit, width), jnp.float32),
            pltpu.VMEM((2, share - 1, UNITS, unit, width), jnp.float32),
            pltpu.VMEM((UNITS, unit, width), jnp.float32),
            dma((2, 2, UNITS)),
            dma((2, 2, UNITS)),
            dma((2, 2, share - 1)),
            dma((2, 2, share - 1)),
            dma((2, KVH, seqs)),
            dma((KVH, seqs)),
            dma((2, share - 1, UNITS)),
            dma((2, share - 1, UNITS)),
            dma((2, UNITS)),
            dma((2, UNITS)),
        ],
        compiler_params=pltpu.CompilerParams(
            collective_id=0, has_side_effects=True, vmem_limit_bytes=56 * 1024 * 1024
        ),
    )(
        tokens.reshape(seqs, SEQ, width),
        student_copy.reshape(UNITS, unit, width),
        snapshot.reshape(UNITS, unit, width),
        cosine,
        sine,
    )
    return gradient.reshape(rows, width)


def per_device(n, blocks, tokens, student_weight, snapshot, moment_one, moment_two):
    master = student_weight[0]
    gradient = gradient_rows(tokens[0], master.astype(jnp.bfloat16), snapshot[0], n, blocks)
    first_new = BETA_ONE * moment_one[0] + (1.0 - BETA_ONE) * gradient
    second_new = BETA_TWO * moment_two[0] + (1.0 - BETA_TWO) * gradient * gradient
    step_dir = (
        first_new
        / (1.0 - BETA_ONE**STEP)
        / (jnp.sqrt(second_new / (1.0 - BETA_TWO**STEP)) + EPSILON)
    )
    updated = master - LEARN_RATE * (step_dir + DECAY * master)
    return (updated[None], first_new[None], second_new[None])


def solution(mesh):
    spec = P("blk", "fsdp", None)
    return jax.shard_map(
        functools.partial(per_device, mesh.shape["fsdp"], mesh.shape["blk"]),
        mesh=mesh,
        in_specs=(spec,) * 5,
        out_specs=(spec,) * 3,
        check_vma=False,
    )
```

```python
import functools
import math

import jax
import jax.numpy as jnp
import numpy as np
from jax import lax
from jax.experimental import pallas as pl
from jax.experimental.pallas import tpu as pltpu
from jax.sharding import PartitionSpec as P

HEADS = 16
KVH = 4
HD = 128
SEQ = 256
STEP = 100
GROUP = HEADS // KVH
HEAD_ROWS = (GROUP + 1) * HD
UNITS = GROUP + 1

THETA = 500000.0
BETA_ONE = 0.9
BETA_TWO = 0.95
LEARN_RATE = 0.002
DECAY = 0.1
EPSILON = 1e-08
MASKED = -1e30
MESH = pl.DeviceIdType.MESH


def rotary_tables():
    positions = np.arange(SEQ, dtype=np.float32)
    exponents = np.arange(HD // 2, dtype=np.float32) * np.float32(2.0 / HD)
    angles = positions[:, None] * (np.float32(THETA) ** (-exponents))[None, :]
    cosine, sine = np.cos(angles), np.sin(angles)
    return (
        np.concatenate([cosine, cosine], axis=1),
        np.concatenate([-sine, sine], axis=1),
    )


def group_grad(x, w_student, w_teacher, cosine, sine):
    inv_root = 1.0 / math.sqrt(HD)

    def project(weight):
        return lax.dot_general(
            x, weight, (((1,), (1,)), ((), ())), preferred_element_type=jnp.float32
        )

    def heads_of(raw):
        parts = []
        for head in range(GROUP + 1):
            part = raw[:, head * HD : (head + 1) * HD]
            turned = part * cosine + pltpu.roll(part, HD // 2, 1) * sine
            parts.append(turned.astype(jnp.bfloat16))
        return parts

    raw_student, raw_teacher = project(w_student), project(w_teacher)
    rows = lax.broadcasted_iota(jnp.int32, (SEQ, SEQ), 0)
    columns = lax.broadcasted_iota(jnp.int32, (SEQ, SEQ), 1)
    causal = rows >= columns

    def probs(query, key):
        scores = (
            lax.dot_general(
                query, key, (((1,), (1,)), ((), ())), preferred_element_type=jnp.float32
            )
            * inv_root
        )
        scores = jnp.where(causal, scores, MASKED)
        spread = jnp.exp(scores - jnp.max(scores, axis=-1, keepdims=True))
        return spread * (1.0 / jnp.sum(spread, axis=-1, keepdims=True))

    def turn_back(part):
        return (part * cosine - pltpu.roll(part, HD // 2, 1) * sine).astype(jnp.bfloat16)

    results = []
    for start in range(0, x.shape[0], SEQ):
        student = heads_of(raw_student[start : start + SEQ])
        teacher = heads_of(raw_teacher[start : start + SEQ])
        pieces = []
        key_grad = jnp.zeros((SEQ, HD), jnp.float32)
        for head in range(GROUP):
            spread = probs(student[head], student[GROUP]) - probs(teacher[head], teacher[GROUP])
            rounded = (jnp.where(causal, spread, 0.0) * (1.0 / HEADS)).astype(jnp.bfloat16)
            query_grad = jnp.dot(rounded, student[GROUP], preferred_element_type=jnp.float32)
            pieces.append(turn_back(query_grad * inv_root))
            key_grad += lax.dot_general(
                rounded, student[head], (((0,), (0,)), ((), ())),
                preferred_element_type=jnp.float32,
            )
        pieces.append(turn_back(key_grad * inv_root))
        results.append(jnp.concatenate(pieces, axis=1))
    return jnp.concatenate(results, axis=0)


def kernel(
    n, blocks, seqs,
    tokens, student, teacher, cos_ref, sin_ref, out,
    held, weight, total, partial, extra,
    w_send, w_recv, s_send, s_recv, t_send, t_recv, g_send, g_recv, f_send, f_recv,
):
    share = n // KVH
    me, blk = lax.axis_index("fsdp"), lax.axis_index("blk")
    chip, lane = lax.div(me, share), lax.rem(me, share)
    last, helper, split = KVH - 1, KVH - 2, KVH - 2

    def placed(native):
        is_key = lax.div(native, HEADS * share)
        key = (native - HEADS * share) * is_key
        head = (1 - is_key) * lax.div(native, GROUP * share) + is_key * lax.div(key, share)
        at = (1 - is_key) * lax.rem(native, GROUP * share) + is_key * (
            GROUP * share + lax.rem(key, share)
        )
        return head * (UNITS * share) + at

    def native_of(place):
        head, at = lax.div(place, UNITS * share), lax.rem(place, UNITS * share)
        is_key = lax.div(at, GROUP * share)
        return (1 - is_key) * (GROUP * share * head + at) + is_key * (
            HEADS * share + share * head + at - GROUP * share
        )

    def each(count, body):
        def run(step, carry):
            body(step)
            return carry

        lax.fori_loop(0, count, run, 0)

    def landed(ref, sem):
        pltpu.make_async_copy(ref, ref, sem).wait()

    def to(src, dst, send_sem, recv_sem, device, group=None):
        target = {"fsdp": device, "blk": blk if group is None else group}
        return pltpu.make_async_remote_copy(
            src_ref=src, dst_ref=dst, send_sem=send_sem, recv_sem=recv_sem,
            device_id=target, device_id_type=MESH,
        )

    for seq in range(seqs):
        pltpu.make_async_copy(tokens.at[seq], held.at[chip, seq], t_recv.at[chip, seq]).start()

    barrier = pltpu.get_barrier_semaphore()
    after = lax.rem(blk + 1, blocks)
    before = lax.rem(blk + blocks - 1, blocks)

    def greet(step):
        pl.semaphore_signal(
            barrier, inc=1, device_id={"fsdp": lax.rem(me + 1 + step, n), "blk": blk},
            device_id_type=MESH,
        )

    def greet_teacher(step):
        pl.semaphore_signal(
            barrier, inc=1, device_id={"fsdp": step, "blk": before}, device_id_type=MESH
        )

    each(n - 1, greet)
    each(n, greet_teacher)
    pl.semaphore_wait(barrier, 2 * n - 1)

    def send_rows(unit, role):
        place = placed(me * UNITS + unit)
        owner, slot = lax.div(place, UNITS), lax.rem(place, UNITS)
        at = lax.rem(place, UNITS * share)

        def send(device):
            @pl.when(device == me)
            def _():
                pltpu.make_async_copy(
                    student.at[unit], weight.at[role, 0, at], w_recv.at[role, 0, slot]
                ).start()

            @pl.when(device != me)
            def _():
                to(
                    student.at[unit], weight.at[role, 0, at], w_send.at[role, 0, unit],
                    w_recv.at[role, 0, slot], device,
                ).start()

            to(
                teacher.at[unit], weight.at[role, 1, at], w_send.at[role, 1, unit],
                w_recv.at[role, 1, slot], device, after,
            ).start()

        if role == 0:
            send(owner)
        else:

            @pl.when(owner >= last * share)
            def _():
                send(owner - share)

    each(UNITS, functools.partial(send_rows, role=0))

    @pl.when(chip < last)
    def _():
        each(UNITS, functools.partial(send_rows, role=1))

    def pass_right(src, slot, seq):
        return to(src, held.at[slot, seq], t_send.at[0, slot, seq], t_recv.at[slot, seq], me + share)

    def pass_left(src, slot, seq):
        return to(src, held.at[slot, seq], t_send.at[1, slot, seq], t_recv.at[slot, seq], me - share)

    def send_own(seq):
        @pl.when(chip < last)
        def _():
            pass_right(tokens.at[seq], chip, seq).start()

        @pl.when(chip > 0)
        def _():
            pass_left(tokens.at[seq], chip, seq).start()

    def own_left(seq):
        @pl.when(chip < last)
        def _():
            landed(held.at[chip, seq], t_send.at[0, chip, seq])

        @pl.when(chip > 0)
        def _():
            landed(held.at[chip, seq], t_send.at[1, chip, seq])

    send_own(0)

    total[...] = jnp.zeros_like(total)

    def sibling(step):
        return chip * share + lax.rem(lane + step, share)

    def share_rows(role, which):
        def arrived(unit):
            landed(weight.at[role, which, lane * UNITS + unit], w_recv.at[role, which, unit])

        each(UNITS, arrived)
        mine = weight.at[role, which, pl.ds(lane * UNITS, UNITS)]
        for step in range(1, share):
            to(
                mine, mine, s_send.at[role, which, step - 1], s_recv.at[role, which, step - 1],
                sibling(step),
            ).start()

    def shared_rows(role, which):
        for step in range(1, share):
            lane_from = lax.rem(lane + share - step, share)
            landed(
                weight.at[role, which, pl.ds(lane_from * UNITS, UNITS)],
                s_recv.at[role, which, step - 1],
            )

    def each_role(body):
        body(0)

        @pl.when(chip == helper)
        def _():
            body(1)

    for which in range(2):
        share_rows(0, which)

    for seq in range(1, seqs):
        own_left(seq - 1)
        send_own(seq)

    @pl.when(chip == last)
    def _():
        landed(held.at[chip, seqs - 1], t_send.at[1, chip, seqs - 1])
        each(UNITS, functools.partial(send_rows, role=1))

    for which in range(2):
        shared_rows(0, which)

    def send_partials(role):
        def send_partial(step):
            unit = UNITS - 1 - step
            for hop in range(1, share):
                lane_to = lax.rem(lane + hop, share)
                to(
                    total.at[role, lane_to * UNITS + unit], partial.at[role, hop - 1, unit],
                    g_send.at[role, hop - 1, unit], g_recv.at[role, hop - 1, unit],
                    sibling(hop),
                ).start()

        each(UNITS, send_partial)

    def send_sums(role):
        landing = (out, extra)[role]

        def send_sum(step):
            unit = UNITS - 1 - step
            at = lane * UNITS + unit
            native = native_of((me + role * share) * UNITS + unit)
            device, slot = lax.div(native, UNITS), lax.rem(native, UNITS)
            for hop in range(1, share):
                landed(partial.at[role, hop - 1, unit], g_recv.at[role, hop - 1, unit])
                total[role, at] += partial[role, hop - 1, unit]

            @pl.when(device == me)
            def _():
                pltpu.make_async_copy(
                    total.at[role, at], landing.at[slot], f_recv.at[role, slot]
                ).start()

            @pl.when(device != me)
            def _():
                to(
                    total.at[role, at], landing.at[slot], f_send.at[role, unit],
                    f_recv.at[role, slot], device,
                ).start()

        each(UNITS, send_sum)

    def chunk(turn):
        distance, side = lax.div(turn + 1, 2), lax.rem(turn, 2)
        slot = chip - distance + 2 * distance * side
        valid = (slot >= 0) & (slot < KVH) & ((chip < last) | (slot >= split))
        relayed = valid & (
            ((side == 1) & (chip > 0)) | ((side == 0) & (distance > 0) & (chip < helper))
        )
        return slot, side, valid, relayed

    def relay(turn, seq):
        slot, side, _, relayed = chunk(turn)

        @pl.when(relayed)
        def _():
            landed(held.at[slot, seq], t_recv.at[slot, seq])

            @pl.when(side == 0)
            def _():
                pass_right(held.at[slot, seq], slot, seq).start()

            @pl.when(side == 1)
            def _():
                pass_left(held.at[slot, seq], slot, seq).start()

    def add_gradient(role, x):
        grad = group_grad(
            x,
            weight[role, 0].reshape(HEAD_ROWS, -1),
            weight[role, 1].reshape(HEAD_ROWS, -1),
            cos_ref[...],
            sin_ref[...],
        )
        width = 512
        for start in range(0, x.shape[1], width):
            piece = lax.dot_general(
                grad, x[:, start : start + width], (((0,), (0,)), ((), ())),
                preferred_element_type=jnp.float32,
            )
            total[role, :, :, start : start + width] += piece.reshape(UNITS * share, -1, width)

    final = 2 * KVH - 3

    def work(turn):
        @pl.when(turn >= 2)
        def _():
            relay(turn + 1, 0)

        slot, _, valid, relayed = chunk(turn)

        @pl.when(valid & (turn < final))
        def _():
            @pl.when(jnp.logical_not(relayed))
            def _():
                each(seqs, lambda seq: landed(held.at[slot, seq], t_recv.at[slot, seq]))

            roles = 1 + lax.div(chip, helper) * lax.div(KVH - 1 - slot, split) * (last - chip)

            def run_role(step):
                role = step + (1 - jnp.minimum(slot, 1)) * (roles - 1 - 2 * step)

                @pl.when((role == 1) & (slot == split - 1))
                def _():
                    for which in range(2):
                        share_rows(1, which)
                    for which in range(2):
                        shared_rows(1, which)

                add_gradient(role, held[slot].reshape(seqs * SEQ, -1))

                @pl.when((role == 1) & (slot == 0))
                def _():
                    send_partials(1)
                    send_sums(1)

            each(roles, run_role)

        @pl.when(valid & (turn >= final))
        def _():
            def run_sequence(seq):
                landed(held.at[slot, seq], t_recv.at[slot, seq])
                add_gradient(0, held[slot, seq])

            each(seqs, run_sequence)

        for seq in range(1, seqs):

            @pl.when(turn >= 2)
            def _():
                relay(turn + 1, seq)

            @pl.when(turn == 0)
            def _():
                relay(2, seq)
                relay(1, seq)

    relay(2, 0)
    relay(1, 0)
    each(2 * KVH - 1, work)

    def sent_tokens(step):
        slot, seq = lax.div(step, seqs), lax.rem(step, seqs)
        later = (slot != chip) | (seq == seqs - 1)

        @pl.when(later & (slot <= chip) & ((chip < helper) | ((chip == helper) & (slot == chip))))
        def _():
            landed(held.at[slot, seq], t_send.at[0, slot, seq])

        @pl.when(later & (slot >= chip) & (chip > 0) & (chip < last))
        def _():
            landed(held.at[slot, seq], t_send.at[1, slot, seq])

    send_partials(0)

    @pl.when(lane < share - 1)
    def _():
        each(KVH * seqs, sent_tokens)

    send_sums(0)

    def arrive(unit):
        landed(out.at[unit], f_recv.at[0, unit])

        @pl.when(placed(me * UNITS + unit) >= last * share * UNITS)
        def _():
            landed(extra.at[unit], f_recv.at[1, unit])
            out[unit] += extra[unit]

    each(UNITS, arrive)

    def sent(unit):
        owner = lax.div(placed(me * UNITS + unit), UNITS)

        def rows_left(role, device):
            @pl.when(device != me)
            def _():
                landed(student.at[unit], w_send.at[role, 0, unit])

            landed(teacher.at[unit], w_send.at[role, 1, unit])

        rows_left(0, owner)

        @pl.when(owner >= last * share)
        def _():
            rows_left(1, owner - share)

        def sums_left(role):
            for step in range(1, share):
                landed(partial.at[role, step - 1, unit], g_send.at[role, step - 1, unit])

            @pl.when(lax.div(native_of((me + role * share) * UNITS + unit), UNITS) != me)
            def _():
                landed(out.at[unit], f_send.at[role, unit])

        each_role(sums_left)

    each(UNITS, sent)

    def shares_left(role):
        for which in range(2):
            for step in range(1, share):
                landed(
                    weight.at[role, which, pl.ds(lane * UNITS, UNITS)],
                    s_send.at[role, which, step - 1],
                )

    each_role(shares_left)

    @pl.when(lane == share - 1)
    def _():
        each(KVH * seqs, sent_tokens)


def gradient_rows(tokens, student_copy, snapshot, n, blocks):
    rows, width = student_copy.shape
    seqs = tokens.shape[0] // SEQ
    share = n // KVH
    unit = rows // UNITS
    cosine, sine = rotary_tables()
    dma = pltpu.SemaphoreType.DMA
    anywhere, vmem = pl.BlockSpec(memory_space=pl.ANY), pl.BlockSpec(memory_space=pltpu.VMEM)
    gradient = pl.pallas_call(
        functools.partial(kernel, n, blocks, seqs),
        out_shape=jax.ShapeDtypeStruct((UNITS, unit, width), jnp.float32),
        in_specs=[anywhere, anywhere, anywhere, vmem, vmem],
        out_specs=vmem,
        scratch_shapes=[
            pltpu.VMEM((KVH, seqs, SEQ, width), jnp.bfloat16),
            pltpu.VMEM((2, 2, UNITS * share, unit, width), jnp.bfloat16),
            pltpu.VMEM((2, UNITS * share, unit, width), jnp.float32),
            pltpu.VMEM((2, share - 1, UNITS, unit, width), jnp.float32),
            pltpu.VMEM((UNITS, unit, width), jnp.float32),
            dma((2, 2, UNITS)),
            dma((2, 2, UNITS)),
            dma((2, 2, share - 1)),
            dma((2, 2, share - 1)),
            dma((2, KVH, seqs)),
            dma((KVH, seqs)),
            dma((2, share - 1, UNITS)),
            dma((2, share - 1, UNITS)),
            dma((2, UNITS)),
            dma((2, UNITS)),
        ],
        compiler_params=pltpu.CompilerParams(
            collective_id=0, has_side_effects=True, vmem_limit_bytes=56 * 1024 * 1024
        ),
    )(
        tokens.reshape(seqs, SEQ, width),
        student_copy.reshape(UNITS, unit, width),
        snapshot.reshape(UNITS, unit, width),
        cosine,
        sine,
    )
    return gradient.reshape(rows, width)


def per_device(n, blocks, tokens, student_weight, snapshot, moment_one, moment_two):
    master = student_weight[0]
    gradient = gradient_rows(tokens[0], master.astype(jnp.bfloat16), snapshot[0], n, blocks)
    first_new = BETA_ONE * moment_one[0] + (1.0 - BETA_ONE) * gradient
    second_new = BETA_TWO * moment_two[0] + (1.0 - BETA_TWO) * gradient * gradient
    step_dir = (
        first_new
        / (1.0 - BETA_ONE**STEP)
        / (jnp.sqrt(second_new / (1.0 - BETA_TWO**STEP)) + EPSILON)
    )
    updated = master - LEARN_RATE * (step_dir + DECAY * master)
    return (updated[None], first_new[None], second_new[None])


def solution(mesh):
    spec = P("blk", "fsdp", None)
    return jax.shard_map(
        functools.partial(per_device, mesh.shape["fsdp"], mesh.shape["blk"]),
        mesh=mesh,
        in_specs=(spec,) * 5,
        out_specs=(spec,) * 3,
        check_vma=False,
    )
```

```python
import functools
import math

import jax
import jax.numpy as jnp
import numpy as np
from jax import lax
from jax.experimental import pallas as pl
from jax.experimental.pallas import tpu as pltpu
from jax.sharding import PartitionSpec as P

HEADS = 16
KVH = 4
HD = 128
SEQ = 256
STEP = 100
GROUP = HEADS // KVH
HEAD_ROWS = (GROUP + 1) * HD
UNITS = GROUP + 1

THETA = 500000.0
BETA_ONE = 0.9
BETA_TWO = 0.95
LEARN_RATE = 0.002
DECAY = 0.1
EPSILON = 1e-08
MASKED = -1e30
MESH = pl.DeviceIdType.MESH


def rotary_tables():
    positions = np.arange(SEQ, dtype=np.float32)
    exponents = np.arange(HD // 2, dtype=np.float32) * np.float32(2.0 / HD)
    angles = positions[:, None] * (np.float32(THETA) ** (-exponents))[None, :]
    cosine, sine = np.cos(angles), np.sin(angles)
    return (
        np.concatenate([cosine, cosine], axis=1),
        np.concatenate([-sine, sine], axis=1),
    )


def group_grad(x, w_student, w_teacher, cosine, sine):
    inv_root = 1.0 / math.sqrt(HD)

    def project(weight):
        return lax.dot_general(
            x, weight, (((1,), (1,)), ((), ())), preferred_element_type=jnp.float32
        )

    def heads_of(raw):
        parts = []
        for head in range(GROUP + 1):
            part = raw[:, head * HD : (head + 1) * HD]
            turned = part * cosine + pltpu.roll(part, HD // 2, 1) * sine
            parts.append(turned.astype(jnp.bfloat16))
        return parts

    raw_student, raw_teacher = project(w_student), project(w_teacher)
    half = SEQ // 2
    base = inv_root * math.log2(math.e)

    def probs(query, key, start):
        stop = start + half
        scores = lax.dot_general(
            query[start:stop], key[:stop], (((1,), (1,)), ((), ())),
            preferred_element_type=jnp.float32,
        )
        rows = lax.broadcasted_iota(jnp.int32, scores.shape, 0) + start
        columns = lax.broadcasted_iota(jnp.int32, scores.shape, 1)
        scores = jnp.where(rows >= columns, scores, MASKED)
        spread = jnp.exp2((scores - jnp.max(scores, axis=-1, keepdims=True)) * base)
        return spread * (1.0 / (HEADS * jnp.sum(spread, axis=-1, keepdims=True)))

    def turn_back(part):
        return (part * cosine - pltpu.roll(part, HD // 2, 1) * sine).astype(jnp.bfloat16)

    results = []
    for start in range(0, x.shape[0], SEQ):
        student = heads_of(raw_student[start : start + SEQ])
        teacher = heads_of(raw_teacher[start : start + SEQ])
        pieces = []
        key_grad = jnp.zeros((SEQ, HD), jnp.float32)
        for head in range(GROUP):
            first, second = (
                (
                    probs(student[head], student[GROUP], begin)
                    - probs(teacher[head], teacher[GROUP], begin)
                ).astype(jnp.bfloat16)
                for begin in (0, half)
            )
            first = jnp.concatenate([first, jnp.zeros_like(first)], axis=1)
            rounded = jnp.concatenate([first, second], axis=0)
            query_grad = jnp.dot(rounded, student[GROUP], preferred_element_type=jnp.float32)
            pieces.append(turn_back(query_grad * inv_root))
            key_grad += lax.dot_general(
                rounded, student[head], (((0,), (0,)), ((), ())),
                preferred_element_type=jnp.float32,
            )
        pieces.append(turn_back(key_grad * inv_root))
        results.append(jnp.concatenate(pieces, axis=1))
    return jnp.concatenate(results, axis=0)


def kernel(
    n, blocks, seqs,
    tokens, student, teacher, cos_ref, sin_ref, out,
    held, weight, total, partial, extra,
    w_send, w_recv, s_send, s_recv, t_send, t_recv, g_send, g_recv, f_send, f_recv,
):
    share = n // KVH
    me, blk = lax.axis_index("fsdp"), lax.axis_index("blk")
    chip, lane = lax.div(me, share), lax.rem(me, share)
    last, helper, split = KVH - 1, KVH - 2, KVH - 2

    def placed(native):
        is_key = lax.div(native, HEADS * share)
        key = (native - HEADS * share) * is_key
        head = (1 - is_key) * lax.div(native, GROUP * share) + is_key * lax.div(key, share)
        at = (1 - is_key) * lax.rem(native, GROUP * share) + is_key * (
            GROUP * share + lax.rem(key, share)
        )
        return head * (UNITS * share) + at

    def native_of(place):
        head, at = lax.div(place, UNITS * share), lax.rem(place, UNITS * share)
        is_key = lax.div(at, GROUP * share)
        return (1 - is_key) * (GROUP * share * head + at) + is_key * (
            HEADS * share + share * head + at - GROUP * share
        )

    def each(count, body):
        def run(step, carry):
            body(step)
            return carry

        lax.fori_loop(0, count, run, 0)

    def landed(ref, sem):
        pltpu.make_async_copy(ref, ref, sem).wait()

    def to(src, dst, send_sem, recv_sem, device, group=None):
        target = {"fsdp": device, "blk": blk if group is None else group}
        return pltpu.make_async_remote_copy(
            src_ref=src, dst_ref=dst, send_sem=send_sem, recv_sem=recv_sem,
            device_id=target, device_id_type=MESH,
        )

    for seq in range(seqs):
        pltpu.make_async_copy(tokens.at[seq], held.at[chip, seq], t_recv.at[chip, seq]).start()

    barrier = pltpu.get_barrier_semaphore()
    after = lax.rem(blk + 1, blocks)
    before = lax.rem(blk + blocks - 1, blocks)

    def greet(step):
        pl.semaphore_signal(
            barrier, inc=1, device_id={"fsdp": lax.rem(me + 1 + step, n), "blk": blk},
            device_id_type=MESH,
        )

    def greet_teacher(step):
        pl.semaphore_signal(
            barrier, inc=1, device_id={"fsdp": step, "blk": before}, device_id_type=MESH
        )

    each(n - 1, greet)
    each(n, greet_teacher)
    pl.semaphore_wait(barrier, 2 * n - 1)

    def send_rows(unit, role):
        place = placed(me * UNITS + unit)
        owner, slot = lax.div(place, UNITS), lax.rem(place, UNITS)
        at = lax.rem(place, UNITS * share)

        def send(device):
            @pl.when(device == me)
            def _():
                pltpu.make_async_copy(
                    student.at[unit], weight.at[role, 0, at], w_recv.at[role, 0, slot]
                ).start()

            @pl.when(device != me)
            def _():
                to(
                    student.at[unit], weight.at[role, 0, at], w_send.at[role, 0, unit],
                    w_recv.at[role, 0, slot], device,
                ).start()

            to(
                teacher.at[unit], weight.at[role, 1, at], w_send.at[role, 1, unit],
                w_recv.at[role, 1, slot], device, after,
            ).start()

        if role == 0:
            send(owner)
        else:

            @pl.when(owner >= last * share)
            def _():
                send(owner - share)

    each(UNITS, functools.partial(send_rows, role=0))

    @pl.when(chip < last)
    def _():
        each(UNITS, functools.partial(send_rows, role=1))

    def pass_right(src, slot, seq):
        return to(src, held.at[slot, seq], t_send.at[0, slot, seq], t_recv.at[slot, seq], me + share)

    def pass_left(src, slot, seq):
        return to(src, held.at[slot, seq], t_send.at[1, slot, seq], t_recv.at[slot, seq], me - share)

    right_passes, left_passes = chip < helper - 1, chip > 1

    def own_right(seq):
        pass_right(tokens.at[seq], chip, seq).start()

    def own_left(seq):
        pass_left(tokens.at[seq], chip, seq).start()

    pl.when(chip < last)(lambda: own_right(0))
    pl.when(chip > 0)(lambda: own_left(0))
    for seq in range(1, seqs):
        pl.when((chip < last) & jnp.logical_not(right_passes))(functools.partial(own_right, seq))
        pl.when((chip > 0) & jnp.logical_not(left_passes))(functools.partial(own_left, seq))

    total[...] = jnp.zeros_like(total)

    def sibling(step):
        return chip * share + lax.rem(lane + step, share)

    def share_rows(role, which):
        def arrived(unit):
            landed(weight.at[role, which, lane * UNITS + unit], w_recv.at[role, which, unit])

        each(UNITS, arrived)
        mine = weight.at[role, which, pl.ds(lane * UNITS, UNITS)]
        for step in range(1, share):
            to(
                mine, mine, s_send.at[role, which, step - 1], s_recv.at[role, which, step - 1],
                sibling(step),
            ).start()

    def shared_rows(role, which):
        for step in range(1, share):
            lane_from = lax.rem(lane + share - step, share)
            landed(
                weight.at[role, which, pl.ds(lane_from * UNITS, UNITS)],
                s_recv.at[role, which, step - 1],
            )

    def each_role(body):
        body(0)

        @pl.when(chip == helper)
        def _():
            body(1)

    for seq in range(1, seqs):

        @pl.when(right_passes)
        def _():
            landed(held.at[chip, seq - 1], t_send.at[0, chip, seq - 1])
            own_right(seq)

        @pl.when(left_passes)
        def _():
            landed(held.at[chip, seq - 1], t_send.at[1, chip, seq - 1])
            own_left(seq)

    for which in range(2):
        share_rows(0, which)

    @pl.when(chip == last)
    def _():
        landed(held.at[chip, seqs - 1], t_send.at[1, chip, seqs - 1])
        each(UNITS, functools.partial(send_rows, role=1))

    for which in range(2):
        shared_rows(0, which)

    def send_partials(role):
        def send_partial(step):
            unit = UNITS - 1 - step
            for hop in range(1, share):
                lane_to = lax.rem(lane + hop, share)
                to(
                    total.at[role, lane_to * UNITS + unit], partial.at[role, hop - 1, unit],
                    g_send.at[role, hop - 1, unit], g_recv.at[role, hop - 1, unit],
                    sibling(hop),
                ).start()

        each(UNITS, send_partial)

    def send_sums(role):
        landing = (out, extra)[role]

        def send_sum(step):
            unit = UNITS - 1 - step
            at = lane * UNITS + unit
            native = native_of((me + role * share) * UNITS + unit)
            device, slot = lax.div(native, UNITS), lax.rem(native, UNITS)
            for hop in range(1, share):
                landed(partial.at[role, hop - 1, unit], g_recv.at[role, hop - 1, unit])
                total[role, at] += partial[role, hop - 1, unit]

            @pl.when(device == me)
            def _():
                pltpu.make_async_copy(
                    total.at[role, at], landing.at[slot], f_recv.at[role, slot]
                ).start()

            @pl.when(device != me)
            def _():
                to(
                    total.at[role, at], landing.at[slot], f_send.at[role, unit],
                    f_recv.at[role, slot], device,
                ).start()

        each(UNITS, send_sum)

    def chunk(turn):
        distance, side = lax.div(turn + 1, 2), lax.rem(turn, 2)
        slot = chip - distance + 2 * distance * side
        valid = (slot >= 0) & (slot < KVH) & ((chip < last) | (slot >= split))
        relayed = valid & (
            ((side == 1) & (chip > 0)) | ((side == 0) & (distance > 0) & (chip < helper))
        )
        return slot, side, valid, relayed

    def relay(turn, seq):
        slot, side, _, relayed = chunk(turn)

        @pl.when(relayed)
        def _():
            landed(held.at[slot, seq], t_recv.at[slot, seq])

            @pl.when(side == 0)
            def _():
                pass_right(held.at[slot, seq], slot, seq).start()

            @pl.when(side == 1)
            def _():
                pass_left(held.at[slot, seq], slot, seq).start()

    def add_gradient(role, x):
        grad = group_grad(
            x,
            weight[role, 0].reshape(HEAD_ROWS, -1),
            weight[role, 1].reshape(HEAD_ROWS, -1),
            cos_ref[...],
            sin_ref[...],
        )
        width = 512
        for start in range(0, x.shape[1], width):
            piece = lax.dot_general(
                grad, x[:, start : start + width], (((0,), (0,)), ((), ())),
                preferred_element_type=jnp.float32,
            )
            total[role, :, :, start : start + width] += piece.reshape(UNITS * share, -1, width)

    final = 2 * KVH - 3

    def work(turn):
        @pl.when(turn >= 2)
        def _():
            relay(turn + 1, 0)

        slot, _, valid, relayed = chunk(turn)

        @pl.when(valid & (turn < final))
        def _():
            @pl.when(jnp.logical_not(relayed))
            def _():
                each(seqs, lambda seq: landed(held.at[slot, seq], t_recv.at[slot, seq]))

            roles = 1 + lax.div(chip, helper) * lax.div(KVH - 1 - slot, split) * (last - chip)

            def run_role(step):
                role = step + (1 - jnp.minimum(slot, 1)) * (roles - 1 - 2 * step)

                @pl.when((role == 1) & (slot == split - 1))
                def _():
                    for which in range(2):
                        share_rows(1, which)
                    for which in range(2):
                        shared_rows(1, which)

                add_gradient(role, held[slot].reshape(seqs * SEQ, -1))

                @pl.when((role == 1) & (slot == 0))
                def _():
                    send_partials(1)
                    send_sums(1)

            each(roles, run_role)

        @pl.when(valid & (turn >= final))
        def _():
            def run_sequence(seq):
                landed(held.at[slot, seq], t_recv.at[slot, seq])
                add_gradient(0, held[slot, seq])

            each(seqs, run_sequence)

        for seq in range(1, seqs):

            @pl.when(turn >= 2)
            def _():
                relay(turn + 1, seq)

            @pl.when(turn == 0)
            def _():
                relay(2, seq)
                relay(1, seq)

    relay(2, 0)
    relay(1, 0)
    each(2 * KVH - 1, work)

    def sent_tokens(step):
        slot, seq = lax.div(step, seqs), lax.rem(step, seqs)
        later = (slot != chip) | (seq == seqs - 1)

        @pl.when((later | jnp.logical_not(right_passes)) & (slot <= chip) & ((chip < helper) | ((chip == helper) & (slot == chip))))
        def _():
            landed(held.at[slot, seq], t_send.at[0, slot, seq])

        @pl.when((later | jnp.logical_not(left_passes)) & (slot >= chip) & (chip > 0) & (chip < last))
        def _():
            landed(held.at[slot, seq], t_send.at[1, slot, seq])

    send_partials(0)

    @pl.when(lane < share - 1)
    def _():
        each(KVH * seqs, sent_tokens)

    send_sums(0)

    def arrive(unit):
        landed(out.at[unit], f_recv.at[0, unit])

        @pl.when(placed(me * UNITS + unit) >= last * share * UNITS)
        def _():
            landed(extra.at[unit], f_recv.at[1, unit])
            out[unit] += extra[unit]

    each(UNITS, arrive)

    def sent(unit):
        owner = lax.div(placed(me * UNITS + unit), UNITS)

        def rows_left(role, device):
            @pl.when(device != me)
            def _():
                landed(student.at[unit], w_send.at[role, 0, unit])

            landed(teacher.at[unit], w_send.at[role, 1, unit])

        rows_left(0, owner)

        @pl.when(owner >= last * share)
        def _():
            rows_left(1, owner - share)

        def sums_left(role):
            for step in range(1, share):
                landed(partial.at[role, step - 1, unit], g_send.at[role, step - 1, unit])

            @pl.when(lax.div(native_of((me + role * share) * UNITS + unit), UNITS) != me)
            def _():
                landed(out.at[unit], f_send.at[role, unit])

        each_role(sums_left)

    each(UNITS, sent)

    def shares_left(role):
        for which in range(2):
            for step in range(1, share):
                landed(
                    weight.at[role, which, pl.ds(lane * UNITS, UNITS)],
                    s_send.at[role, which, step - 1],
                )

    each_role(shares_left)

    @pl.when(lane == share - 1)
    def _():
        each(KVH * seqs, sent_tokens)


def gradient_rows(tokens, student_copy, snapshot, n, blocks):
    rows, width = student_copy.shape
    seqs = tokens.shape[0] // SEQ
    share = n // KVH
    unit = rows // UNITS
    cosine, sine = rotary_tables()
    dma = pltpu.SemaphoreType.DMA
    anywhere, vmem = pl.BlockSpec(memory_space=pl.ANY), pl.BlockSpec(memory_space=pltpu.VMEM)
    gradient = pl.pallas_call(
        functools.partial(kernel, n, blocks, seqs),
        out_shape=jax.ShapeDtypeStruct((UNITS, unit, width), jnp.float32),
        in_specs=[anywhere, anywhere, anywhere, vmem, vmem],
        out_specs=vmem,
        scratch_shapes=[
            pltpu.VMEM((KVH, seqs, SEQ, width), jnp.bfloat16),
            pltpu.VMEM((2, 2, UNITS * share, unit, width), jnp.bfloat16),
            pltpu.VMEM((2, UNITS * share, unit, width), jnp.float32),
            pltpu.VMEM((2, share - 1, UNITS, unit, width), jnp.float32),
            pltpu.VMEM((UNITS, unit, width), jnp.float32),
            dma((2, 2, UNITS)),
            dma((2, 2, UNITS)),
            dma((2, 2, share - 1)),
            dma((2, 2, share - 1)),
            dma((2, KVH, seqs)),
            dma((KVH, seqs)),
            dma((2, share - 1, UNITS)),
            dma((2, share - 1, UNITS)),
            dma((2, UNITS)),
            dma((2, UNITS)),
        ],
        compiler_params=pltpu.CompilerParams(
            collective_id=0, has_side_effects=True, vmem_limit_bytes=56 * 1024 * 1024
        ),
    )(
        tokens.reshape(seqs, SEQ, width),
        student_copy.reshape(UNITS, unit, width),
        snapshot.reshape(UNITS, unit, width),
        cosine,
        sine,
    )
    return gradient.reshape(rows, width)


def per_device(n, blocks, tokens, student_weight, snapshot, moment_one, moment_two):
    master = student_weight[0]
    gradient = gradient_rows(tokens[0], master.astype(jnp.bfloat16), snapshot[0], n, blocks)
    first_new = BETA_ONE * moment_one[0] + (1.0 - BETA_ONE) * gradient
    second_new = BETA_TWO * moment_two[0] + (1.0 - BETA_TWO) * gradient * gradient
    step_dir = (
        first_new
        / (1.0 - BETA_ONE**STEP)
        / (jnp.sqrt(second_new / (1.0 - BETA_TWO**STEP)) + EPSILON)
    )
    updated = master - LEARN_RATE * (step_dir + DECAY * master)
    return (updated[None], first_new[None], second_new[None])


def solution(mesh):
    spec = P("blk", "fsdp", None)
    return jax.shard_map(
        functools.partial(per_device, mesh.shape["fsdp"], mesh.shape["blk"]),
        mesh=mesh,
        in_specs=(spec,) * 5,
        out_specs=(spec,) * 3,
        check_vma=False,
    )
```

```python
import functools
import math

import jax
import jax.numpy as jnp
import numpy as np
from jax import lax
from jax.experimental import pallas as pl
from jax.experimental.pallas import tpu as pltpu
from jax.sharding import PartitionSpec as P

HEADS = 16
KVH = 4
HD = 128
SEQ = 256
STEP = 100
GROUP = HEADS // KVH
HEAD_ROWS = (GROUP + 1) * HD
UNITS = GROUP + 1

THETA = 500000.0
BETA_ONE = 0.9
BETA_TWO = 0.95
LEARN_RATE = 0.002
DECAY = 0.1
EPSILON = 1e-08
MASKED = -1e30
MESH = pl.DeviceIdType.MESH


def rotary_tables():
    positions = np.arange(SEQ, dtype=np.float32)
    exponents = np.arange(HD // 2, dtype=np.float32) * np.float32(2.0 / HD)
    angles = positions[:, None] * (np.float32(THETA) ** (-exponents))[None, :]
    cosine, sine = np.cos(angles), np.sin(angles)
    return (
        np.concatenate([cosine, cosine], axis=1),
        np.concatenate([-sine, sine], axis=1),
    )


def group_grad(x, w_student, w_teacher, cosine, sine):
    inv_root = 1.0 / math.sqrt(HD)

    def project(weight):
        return lax.dot_general(
            x, weight, (((1,), (1,)), ((), ())), preferred_element_type=jnp.float32
        )

    def heads_of(raw):
        parts = []
        for head in range(GROUP + 1):
            part = raw[:, head * HD : (head + 1) * HD]
            turned = part * cosine + pltpu.roll(part, HD // 2, 1) * sine
            parts.append(turned.astype(jnp.bfloat16))
        return parts

    raw_student, raw_teacher = project(w_student), project(w_teacher)
    half = SEQ // 2
    base = inv_root * math.log2(math.e)

    def probs(query, key, start):
        stop = start + half
        scores = lax.dot_general(
            query[start:stop], key[:stop], (((1,), (1,)), ((), ())),
            preferred_element_type=jnp.float32,
        )
        rows = lax.broadcasted_iota(jnp.int32, scores.shape, 0) + start
        columns = lax.broadcasted_iota(jnp.int32, scores.shape, 1)
        scores = jnp.where(rows >= columns, scores, MASKED)
        spread = jnp.exp2((scores - jnp.max(scores, axis=-1, keepdims=True)) * base)
        return spread * (1.0 / (HEADS * jnp.sum(spread, axis=-1, keepdims=True)))

    def turn_back(part):
        return (part * cosine - pltpu.roll(part, HD // 2, 1) * sine).astype(jnp.bfloat16)

    results = []
    for start in range(0, x.shape[0], SEQ):
        student = heads_of(raw_student[start : start + SEQ])
        teacher = heads_of(raw_teacher[start : start + SEQ])
        pieces = []
        key_grad = jnp.zeros((SEQ, HD), jnp.float32)
        for head in range(GROUP):
            first, second = (
                (
                    probs(student[head], student[GROUP], begin)
                    - probs(teacher[head], teacher[GROUP], begin)
                ).astype(jnp.bfloat16)
                for begin in (0, half)
            )
            first = jnp.concatenate([first, jnp.zeros_like(first)], axis=1)
            rounded = jnp.concatenate([first, second], axis=0)
            query_grad = jnp.dot(rounded, student[GROUP], preferred_element_type=jnp.float32)
            pieces.append(turn_back(query_grad * inv_root))
            key_grad += lax.dot_general(
                rounded, student[head], (((0,), (0,)), ((), ())),
                preferred_element_type=jnp.float32,
            )
        pieces.append(turn_back(key_grad * inv_root))
        results.append(jnp.concatenate(pieces, axis=1))
    return jnp.concatenate(results, axis=0)


def kernel(
    n, blocks, seqs,
    tokens, student, teacher, cos_ref, sin_ref, out,
    held, weight, total, partial, extra,
    w_send, w_recv, s_send, s_recv, t_send, t_recv, g_send, g_recv, f_send, f_recv,
):
    share = n // KVH
    me, blk = lax.axis_index("fsdp"), lax.axis_index("blk")
    chip, lane = lax.div(me, share), lax.rem(me, share)
    last, helper, split = KVH - 1, KVH - 2, KVH - 2

    def placed(native):
        is_key = lax.div(native, HEADS * share)
        key = (native - HEADS * share) * is_key
        head = (1 - is_key) * lax.div(native, GROUP * share) + is_key * lax.div(key, share)
        at = (1 - is_key) * lax.rem(native, GROUP * share) + is_key * (
            GROUP * share + lax.rem(key, share)
        )
        return head * (UNITS * share) + at

    def native_of(place):
        head, at = lax.div(place, UNITS * share), lax.rem(place, UNITS * share)
        is_key = lax.div(at, GROUP * share)
        return (1 - is_key) * (GROUP * share * head + at) + is_key * (
            HEADS * share + share * head + at - GROUP * share
        )

    def each(count, body):
        def run(step, carry):
            body(step)
            return carry

        lax.fori_loop(0, count, run, 0)

    def landed(ref, sem):
        pltpu.make_async_copy(ref, ref, sem).wait()

    def to(src, dst, send_sem, recv_sem, device, group=None):
        target = {"fsdp": device, "blk": blk if group is None else group}
        return pltpu.make_async_remote_copy(
            src_ref=src, dst_ref=dst, send_sem=send_sem, recv_sem=recv_sem,
            device_id=target, device_id_type=MESH,
        )

    for seq in range(seqs):
        pltpu.make_async_copy(tokens.at[seq], held.at[chip, seq], t_recv.at[chip, seq]).start()

    barrier = pltpu.get_barrier_semaphore()
    after = lax.rem(blk + 1, blocks)
    before = lax.rem(blk + blocks - 1, blocks)

    def greet(step):
        pl.semaphore_signal(
            barrier, inc=1, device_id={"fsdp": lax.rem(me + 1 + step, n), "blk": blk},
            device_id_type=MESH,
        )

    def greet_teacher(step):
        pl.semaphore_signal(
            barrier, inc=1, device_id={"fsdp": step, "blk": before}, device_id_type=MESH
        )

    each(n - 1, greet)
    each(n, greet_teacher)
    pl.semaphore_wait(barrier, 2 * n - 1)

    def send_rows(unit, role):
        place = placed(me * UNITS + unit)
        owner, slot = lax.div(place, UNITS), lax.rem(place, UNITS)
        at = lax.rem(place, UNITS * share)

        def send(device):
            @pl.when(device == me)
            def _():
                pltpu.make_async_copy(
                    student.at[unit], weight.at[role, 0, at], w_recv.at[role, 0, slot]
                ).start()

            @pl.when(device != me)
            def _():
                to(
                    student.at[unit], weight.at[role, 0, at], w_send.at[role, 0, unit],
                    w_recv.at[role, 0, slot], device,
                ).start()

            to(
                teacher.at[unit], weight.at[role, 1, at], w_send.at[role, 1, unit],
                w_recv.at[role, 1, slot], device, after,
            ).start()

        if role == 0:
            send(owner)
        else:

            @pl.when(owner >= last * share)
            def _():
                send(owner - share)

    each(UNITS, functools.partial(send_rows, role=0))

    @pl.when(chip < last)
    def _():
        each(UNITS, functools.partial(send_rows, role=1))

    def pass_right(src, slot, seq):
        return to(src, held.at[slot, seq], t_send.at[0, slot, seq], t_recv.at[slot, seq], me + share)

    def pass_left(src, slot, seq):
        return to(src, held.at[slot, seq], t_send.at[1, slot, seq], t_recv.at[slot, seq], me - share)

    right_passes, left_passes = chip < helper - 1, chip > 1

    def own_right(seq):
        pass_right(tokens.at[seq], chip, seq).start()

    def own_left(seq):
        pass_left(tokens.at[seq], chip, seq).start()

    pl.when(chip < last)(lambda: own_right(0))
    pl.when(chip > 0)(lambda: own_left(0))
    for seq in range(1, seqs):
        pl.when((chip < last) & jnp.logical_not(right_passes))(functools.partial(own_right, seq))
        pl.when((chip > 0) & jnp.logical_not(left_passes))(functools.partial(own_left, seq))

    total[...] = jnp.zeros_like(total)

    def sibling(step):
        return chip * share + lax.rem(lane + step, share)

    def share_rows(role, which):
        def arrived(unit):
            landed(weight.at[role, which, lane * UNITS + unit], w_recv.at[role, which, unit])

        each(UNITS, arrived)
        mine = weight.at[role, which, pl.ds(lane * UNITS, UNITS)]
        for step in range(1, share):
            to(
                mine, mine, s_send.at[role, which, step - 1], s_recv.at[role, which, step - 1],
                sibling(step),
            ).start()

    def shared_rows(role, which):
        for step in range(1, share):
            lane_from = lax.rem(lane + share - step, share)
            landed(
                weight.at[role, which, pl.ds(lane_from * UNITS, UNITS)],
                s_recv.at[role, which, step - 1],
            )

    def each_role(body):
        body(0)

        @pl.when(chip == helper)
        def _():
            body(1)

    for seq in range(1, seqs):

        @pl.when(right_passes)
        def _():
            landed(held.at[chip, seq - 1], t_send.at[0, chip, seq - 1])
            own_right(seq)

        @pl.when(left_passes)
        def _():
            landed(held.at[chip, seq - 1], t_send.at[1, chip, seq - 1])
            own_left(seq)

    for which in range(2):
        share_rows(0, which)

    @pl.when(chip == last)
    def _():
        landed(held.at[chip, seqs - 1], t_send.at[1, chip, seqs - 1])
        each(UNITS, functools.partial(send_rows, role=1))

    for which in range(2):
        shared_rows(0, which)

    def send_partials(role):
        def send_partial(step):
            unit = UNITS - 1 - step
            for hop in range(1, share):
                lane_to = lax.rem(lane + hop, share)
                to(
                    total.at[role, lane_to * UNITS + unit], partial.at[role, hop - 1, unit],
                    g_send.at[role, hop - 1, unit], g_recv.at[role, hop - 1, unit],
                    sibling(hop),
                ).start()

        each(UNITS, send_partial)

    def send_sums(role):
        landing = (out, extra)[role]

        def send_sum(step):
            unit = UNITS - 1 - step
            at = lane * UNITS + unit
            native = native_of((me + role * share) * UNITS + unit)
            device, slot = lax.div(native, UNITS), lax.rem(native, UNITS)
            for hop in range(1, share):
                landed(partial.at[role, hop - 1, unit], g_recv.at[role, hop - 1, unit])
                total[role, at] += partial[role, hop - 1, unit]

            @pl.when(device == me)
            def _():
                pltpu.make_async_copy(
                    total.at[role, at], landing.at[slot], f_recv.at[role, slot]
                ).start()

            @pl.when(device != me)
            def _():
                to(
                    total.at[role, at], landing.at[slot], f_send.at[role, unit],
                    f_recv.at[role, slot], device,
                ).start()

        each(UNITS, send_sum)

    def chunk(turn):
        distance, side = lax.div(turn + 1, 2), lax.rem(turn, 2)
        slot = chip - distance + 2 * distance * side
        valid = (slot >= 0) & (slot < KVH) & ((chip < last) | (slot >= split))
        relayed = valid & (
            ((side == 1) & (chip > 0)) | ((side == 0) & (distance > 0) & (chip < helper))
        )
        return slot, side, valid, relayed

    def relay(turn, seq):
        slot, side, _, relayed = chunk(turn)

        @pl.when(relayed)
        def _():
            landed(held.at[slot, seq], t_recv.at[slot, seq])

            @pl.when(side == 0)
            def _():
                pass_right(held.at[slot, seq], slot, seq).start()

            @pl.when(side == 1)
            def _():
                pass_left(held.at[slot, seq], slot, seq).start()

    def add_gradient(role, x):
        grad = group_grad(
            x,
            weight[role, 0].reshape(HEAD_ROWS, -1),
            weight[role, 1].reshape(HEAD_ROWS, -1),
            cos_ref[...],
            sin_ref[...],
        )
        turned = grad.T
        width = 512
        for start in range(0, x.shape[1], width):
            piece = lax.dot_general(
                turned, x[:, start : start + width], (((1,), (0,)), ((), ())),
                preferred_element_type=jnp.float32,
            )
            total[role, :, :, start : start + width] += piece.reshape(UNITS * share, -1, width)

    final = 2 * KVH - 3

    def work(turn):
        @pl.when(turn >= 2)
        def _():
            relay(turn + 1, 0)

        slot, _, valid, relayed = chunk(turn)

        @pl.when(valid & (turn < final))
        def _():
            @pl.when(jnp.logical_not(relayed))
            def _():
                each(seqs, lambda seq: landed(held.at[slot, seq], t_recv.at[slot, seq]))

            roles = 1 + lax.div(chip, helper) * lax.div(KVH - 1 - slot, split) * (last - chip)

            def run_role(step):
                role = step + (1 - jnp.minimum(slot, 1)) * (roles - 1 - 2 * step)

                @pl.when((role == 1) & (slot == split - 1))
                def _():
                    for which in range(2):
                        share_rows(1, which)
                    for which in range(2):
                        shared_rows(1, which)

                add_gradient(role, held[slot].reshape(seqs * SEQ, -1))

                @pl.when((role == 1) & (slot == 0))
                def _():
                    send_partials(1)
                    send_sums(1)

            each(roles, run_role)

        @pl.when(valid & (turn >= final))
        def _():
            def run_sequence(seq):
                landed(held.at[slot, seq], t_recv.at[slot, seq])
                add_gradient(0, held[slot, seq])

            each(seqs, run_sequence)

        for seq in range(1, seqs):

            @pl.when(turn >= 2)
            def _():
                relay(turn + 1, seq)

            @pl.when(turn == 0)
            def _():
                relay(2, seq)
                relay(1, seq)

    relay(2, 0)
    relay(1, 0)
    each(2 * KVH - 1, work)

    def sent_tokens(step):
        slot, seq = lax.div(step, seqs), lax.rem(step, seqs)
        later = (slot != chip) | (seq == seqs - 1)

        @pl.when((later | jnp.logical_not(right_passes)) & (slot <= chip) & ((chip < helper) | ((chip == helper) & (slot == chip))))
        def _():
            landed(held.at[slot, seq], t_send.at[0, slot, seq])

        @pl.when((later | jnp.logical_not(left_passes)) & (slot >= chip) & (chip > 0) & (chip < last))
        def _():
            landed(held.at[slot, seq], t_send.at[1, slot, seq])

    send_partials(0)

    @pl.when(lane < share - 1)
    def _():
        each(KVH * seqs, sent_tokens)

    send_sums(0)

    def arrive(unit):
        landed(out.at[unit], f_recv.at[0, unit])

        @pl.when(placed(me * UNITS + unit) >= last * share * UNITS)
        def _():
            landed(extra.at[unit], f_recv.at[1, unit])
            out[unit] += extra[unit]

    each(UNITS, arrive)

    def sent(unit):
        owner = lax.div(placed(me * UNITS + unit), UNITS)

        def rows_left(role, device):
            @pl.when(device != me)
            def _():
                landed(student.at[unit], w_send.at[role, 0, unit])

            landed(teacher.at[unit], w_send.at[role, 1, unit])

        rows_left(0, owner)

        @pl.when(owner >= last * share)
        def _():
            rows_left(1, owner - share)

        def sums_left(role):
            for step in range(1, share):
                landed(partial.at[role, step - 1, unit], g_send.at[role, step - 1, unit])

            @pl.when(lax.div(native_of((me + role * share) * UNITS + unit), UNITS) != me)
            def _():
                landed(out.at[unit], f_send.at[role, unit])

        each_role(sums_left)

    each(UNITS, sent)

    def shares_left(role):
        for which in range(2):
            for step in range(1, share):
                landed(
                    weight.at[role, which, pl.ds(lane * UNITS, UNITS)],
                    s_send.at[role, which, step - 1],
                )

    each_role(shares_left)

    @pl.when(lane == share - 1)
    def _():
        each(KVH * seqs, sent_tokens)


def gradient_rows(tokens, student_copy, snapshot, n, blocks):
    rows, width = student_copy.shape
    seqs = tokens.shape[0] // SEQ
    share = n // KVH
    unit = rows // UNITS
    cosine, sine = rotary_tables()
    dma = pltpu.SemaphoreType.DMA
    anywhere, vmem = pl.BlockSpec(memory_space=pl.ANY), pl.BlockSpec(memory_space=pltpu.VMEM)
    gradient = pl.pallas_call(
        functools.partial(kernel, n, blocks, seqs),
        out_shape=jax.ShapeDtypeStruct((UNITS, unit, width), jnp.float32),
        in_specs=[anywhere, anywhere, anywhere, vmem, vmem],
        out_specs=vmem,
        scratch_shapes=[
            pltpu.VMEM((KVH, seqs, SEQ, width), jnp.bfloat16),
            pltpu.VMEM((2, 2, UNITS * share, unit, width), jnp.bfloat16),
            pltpu.VMEM((2, UNITS * share, unit, width), jnp.float32),
            pltpu.VMEM((2, share - 1, UNITS, unit, width), jnp.float32),
            pltpu.VMEM((UNITS, unit, width), jnp.float32),
            dma((2, 2, UNITS)),
            dma((2, 2, UNITS)),
            dma((2, 2, share - 1)),
            dma((2, 2, share - 1)),
            dma((2, KVH, seqs)),
            dma((KVH, seqs)),
            dma((2, share - 1, UNITS)),
            dma((2, share - 1, UNITS)),
            dma((2, UNITS)),
            dma((2, UNITS)),
        ],
        compiler_params=pltpu.CompilerParams(
            collective_id=0, has_side_effects=True, vmem_limit_bytes=56 * 1024 * 1024
        ),
    )(
        tokens.reshape(seqs, SEQ, width),
        student_copy.reshape(UNITS, unit, width),
        snapshot.reshape(UNITS, unit, width),
        cosine,
        sine,
    )
    return gradient.reshape(rows, width)


def per_device(n, blocks, tokens, student_weight, snapshot, moment_one, moment_two):
    master = student_weight[0]
    gradient = gradient_rows(tokens[0], master.astype(jnp.bfloat16), snapshot[0], n, blocks)
    first_new = BETA_ONE * moment_one[0] + (1.0 - BETA_ONE) * gradient
    second_new = BETA_TWO * moment_two[0] + (1.0 - BETA_TWO) * gradient * gradient
    step_dir = (
        first_new
        / (1.0 - BETA_ONE**STEP)
        / (jnp.sqrt(second_new / (1.0 - BETA_TWO**STEP)) + EPSILON)
    )
    updated = master - LEARN_RATE * (step_dir + DECAY * master)
    return (updated[None], first_new[None], second_new[None])


def solution(mesh):
    spec = P("blk", "fsdp", None)
    return jax.shard_map(
        functools.partial(per_device, mesh.shape["fsdp"], mesh.shape["blk"]),
        mesh=mesh,
        in_specs=(spec,) * 5,
        out_specs=(spec,) * 3,
        check_vma=False,
    )
```
